256 devices in a mesh: layer: 32 (over x, y, core), feat: 8 (over z).
Axes of the slice: x: 4, y: 4, z: 8, core: 2. Of those that a mesh axis runs over, the one named last changes fastest.
Arguments:
- cotangent: bfloat16 [2, 1024, 5120], P(None, 'layer', 'feat'), may hold values from -6 to 6
- decoder: bfloat16 [65536, 2, 5120], P(('layer', 'feat')), may hold values from -0.0625 to 0.0625
- encoder: bfloat16 [5120, 65536], P(None, ('layer', 'feat')), may hold values from -0.375 to 0.375
- preact: bfloat16 [1024, 65536], P(None, ('layer', 'feat')), may hold values from -6 to 6
- block_ids: int32 [2, 16, 32], replicated, may hold values from 0 to 255, as said below
- block_counts: int32 [2, 16], replicated, may hold values from 8 to 32, as said below
Outputs:
- feature_grad: bfloat16 [1024, 65536], P(None, ('layer', 'feat'))
- input_grad: bfloat16 [2, 1024, 5120], P(None, 'layer', 'feat')
The draws below stay inside these ranges and needn't reach their ends.
Inputs may be any that keep to these rules, and one draw needn't show every extreme that they name: `block_ids`: within one list the entries are distinct block numbers; entries past the count are valid numbers and are ignored. `block_counts`: the count 32 is reached by some list in every draw.
All inputs are finite; a program needn't handle non-finite values.
Results may differ from the reference program's by a relative error of at most 0.005.
Values may be sent and summed in bfloat16 or wider, within the bound.
A program may use at most 128 MiB of HBM per device.

```python
import jax
import jax.numpy as jnp

D = 5120
F = 32768
LAYERS = 2
TOK = 1024
WIN = 64
ACTIVE = 32
NWIN = 16
BLOCKS = 256


def draw_block_ids(key, part):
    key = jax.random.fold_in(key, 11)
    keys = jax.random.split(key, LAYERS * NWIN)
    orders = jax.vmap(lambda single: jax.random.permutation(single, BLOCKS))(keys)
    return orders[:, :ACTIVE].reshape(LAYERS, NWIN, ACTIVE).astype(jnp.int32)


def draw_block_counts(key, part):
    key = jax.random.fold_in(key, 23)
    first, second = jax.random.split(key)
    counts = jax.random.randint(first, (LAYERS * NWIN,), ACTIVE // 4, ACTIVE + 1)
    where_full = jax.random.randint(second, (), 0, LAYERS * NWIN)
    counts = jnp.where(jnp.arange(LAYERS * NWIN) == where_full, ACTIVE, counts)
    return counts.reshape(LAYERS, NWIN).astype(jnp.int32)


def with_spikes(values, key, source, target, parts, factor):
    def block_of(axis_at):
        return (jnp.arange(values.shape[axis_at]) // (values.shape[axis_at] // parts)).reshape((-1,) + (1,) * (values.ndim - 1 - axis_at))

    near = jax.random.permutation(key, parts)[block_of(target)]
    other_side = (block_of(target) + parts // 2) % parts
    return jnp.where((block_of(source) == near) | (block_of(source) == other_side), factor * values, values)


def level_of(own_key, dims, shards, smallest, high):
    def one(position, blocks):
        draws = jax.random.uniform(jax.random.fold_in(jax.random.fold_in(own_key, 6), position), (blocks,), jnp.float32, smallest / len(shards), high / len(shards))
        return jnp.repeat(jnp.exp(draws), dims[position] // blocks).reshape((-1,) + (1,) * (len(dims) - position - 1))

    gain = one(*shards[0])
    for cut in shards[1:]:
        gain = gain * one(*cut)
    return gain


def centred(own_key, dims, deviation, most, pieces=(), dtype=jnp.bfloat16):
    result = deviation * jax.random.normal(own_key, dims, jnp.float32)
    if pieces:
        result = result * level_of(own_key, dims, pieces, -0.22, 0.18)
    return jnp.clip(result, -most, most).astype(dtype)


def noise_with(rng, dims, width, most, pieces, heavy, kind=jnp.bfloat16):
    values = width * jax.random.normal(rng, dims, jnp.float32)
    if pieces:
        values = values * level_of(rng, dims, pieces, -0.22, 0.18)
    return jnp.clip(with_spikes(values, jax.random.fold_in(rng, 3), *heavy), -most, most).astype(kind)


def setup_inputs(seed: int = 0) -> dict:
    splits = jax.random.split(jax.random.key(seed), 7)
    cotangent = centred(splits[0], (LAYERS, TOK, D), 1.0, 6.0, ((1, 32), (2, 8)))
    decoder = centred(splits[1], (LAYERS * F, LAYERS, D), (D * LAYERS) ** -0.5, 0.0625, ((0, 256),))
    encoder = noise_with(splits[2], (D, LAYERS * F), (F // 8) ** -0.5, 0.375, ((1, 256),), (1, 0, 256, 6.0))
    preact = centred(splits[3], (TOK, LAYERS * F), 1.0, 6.0, ((1, 256),))
    block_ids = draw_block_ids(jax.random.fold_in(splits[6], 71), 0)
    block_counts = draw_block_counts(jax.random.fold_in(splits[6], 71), 0)
    return dict(cotangent=cotangent, decoder=decoder, encoder=encoder, preact=preact, block_ids=block_ids, block_counts=block_counts)


def window_mask(block_ids, block_counts, source):
    live_slots = jnp.arange(ACTIVE)[None, :] < block_counts[source][:, None]
    matches = block_ids[source][:, :, None] == jnp.arange(BLOCKS)[None, None, :]
    blockhit = jnp.any(matches & live_slots[:, :, None], axis=1)
    spread = jnp.broadcast_to(blockhit[:, None, :, None], (NWIN, WIN, BLOCKS, 128))
    return spread.reshape(TOK, F)


def reference(cotangent, decoder, encoder, preact, block_ids, block_counts):
    grads = []
    inputs = []
    for source in range(LAYERS):
        total = jnp.zeros((TOK, F), jnp.float32)
        for target in range(source, LAYERS):
            weights = decoder[source * F:(source + 1) * F, target, :]
            total = total + jnp.dot(cotangent[target], weights.T, preferred_element_type=jnp.float32)
        active = window_mask(block_ids, block_counts, source) & (preact[:, source * F:(source + 1) * F] > 0)
        gradient = jnp.where(active, total, 0.0).astype(jnp.bfloat16)
        grads.append(gradient)
        columns = encoder[:, source * F:(source + 1) * F]
        inputs.append(jnp.dot(gradient, columns.T, preferred_element_type=jnp.float32).astype(jnp.bfloat16))
    return jnp.concatenate(grads, axis=1), jnp.stack(inputs, axis=0)
```

```python
import functools

import jax
import jax.numpy as jnp
from jax import lax
from jax.experimental import pallas as pl
from jax.experimental.pallas import tpu as pltpu
from jax.sharding import PartitionSpec as P

MESH = pl.DeviceIdType.MESH
WIN = 64
ROWS = WIN // 2
HALF = ROWS // 2
BLOCK = 128
F32 = jnp.float32
BF16 = jnp.bfloat16


class Semaphores:
    def __init__(self, send, recv):
        self.send, self.recv, self.used = send, recv, 0

    def take(self, count=1):
        first = self.used
        self.used += count
        return first

    def copy(self, source, target, index, device):
        return pltpu.make_async_remote_copy(
            src_ref=source,
            dst_ref=target,
            send_sem=self.send.at[index],
            recv_sem=self.recv.at[index],
            device_id=device,
            device_id_type=MESH,
        )


def both(index):
    return pl.ds(index * HALF, HALF)


def ring_gather(sems, n, me, right, left, chunk, subs, drains):
    steps = n // 2
    base = sems.take(steps * 2 * subs)
    sides = ((right, -1), (left, 1))

    def copies(step, sub, sent):
        last = step == steps
        found = []
        for side, (device, sign) in enumerate(sides):
            at = lax.rem(me + (n + sign * (step - (1 if sent else 0))), n)
            rows = both(side) if last else pl.ds(0, ROWS)
            ref = chunk(at, sub, rows)
            found.append(sems.copy(ref, ref, base + ((step - 1) * 2 + side) * subs + sub, device))
        return found

    def over(fn):
        if subs == 1:
            fn(0)
        else:
            def loop(sub, carry):
                fn(sub)
                return carry

            lax.fori_loop(0, subs, loop, 0)

    def stage(step):
        def run():
            def one(sub):
                if step > 1:
                    for copy in copies(step - 1, sub, False):
                        copy.wait_recv()
                if step <= steps:
                    for copy in copies(step, sub, True):
                        copy.start()

            over(one)

        return run

    def drain():
        for step in range(1, steps + 1):
            def one(sub):
                for copy in copies(step, sub, True):
                    copy.wait_send()

            over(one)

    drains.append(drain)
    return [stage(step) for step in range(1, steps + 2)]


def ring_scatter(sems, n, me, right, left, own, outer, inner, bufs, drains):
    half_send, half_recv, full_send, full_recv = bufs
    steps = n // 2
    base = sems.take(steps * 2 * outer)
    sides = ((right, 1), (left, -1))

    def copy_of(step, side, o):
        device = sides[side][0]
        index = base + ((step - 1) * 2 + side) * outer + o
        if step == 1:
            return sems.copy(half_send.at[side, o], half_recv.at[side, o], index, device)
        return sems.copy(full_send.at[step - 2, side, o], full_recv.at[step - 2, side, o], index, device)

    def loop_inner(fn):
        if inner == 1:
            fn(0)
        else:
            def loop(j, carry):
                fn(j)
                return carry

            lax.fori_loop(0, inner, loop, 0)

    def stage(step):
        def one(o, carry):
            for side, (_, sign) in enumerate(sides):
                at = lax.rem(me + (n + sign * (steps - step + 1)), n)
                if step > 1:
                    copy_of(step - 1, side, o).wait_recv()

                def add(j):
                    if step == 1:
                        half_send[side, o, j] = own(at, o, j)[pl.ds(side * HALF, HALF), :].astype(BF16)
                    elif step == 2:
                        mine = pl.ds(side * HALF, HALF)
                        other = pl.ds((1 - side) * HALF, HALF)
                        ref = own(at, o, j)
                        full_send[step - 2, side, o, j, mine, :] = (
                            ref[mine, :] + half_recv[side, o, j].astype(F32)
                        ).astype(BF16)
                        full_send[step - 2, side, o, j, other, :] = ref[other, :].astype(BF16)
                    else:
                        full_send[step - 2, side, o, j] = (
                            own(at, o, j)[...] + full_recv[step - 3, side, o, j].astype(F32)
                        ).astype(BF16)

                loop_inner(add)
                copy_of(step, side, o).start()
            return carry

        return lambda: lax.fori_loop(0, outer, one, 0)

    def final():
        def one(o, carry):
            for side in range(2):
                copy_of(steps, side, o).wait_recv()

            def add(j):
                ref = own(me, o, j)
                if steps == 1:
                    for side in range(2):
                        mine = pl.ds(side * HALF, HALF)
                        ref[mine, :] = ref[mine, :] + half_recv[side, o, j].astype(F32)
                else:
                    ref[...] = (
                        ref[...]
                        + full_recv[steps - 2, 0, o, j].astype(F32)
                        + full_recv[steps - 2, 1, o, j].astype(F32)
                    )

            loop_inner(add)
            return carry

        lax.fori_loop(0, outer, one, 0)

    def drain():
        for step in range(1, steps + 1):
            def one(o, carry):
                for side in range(2):
                    copy_of(step, side, o).wait_send()
                return carry

            lax.fori_loop(0, outer, one, 0)

    drains.append(drain)
    return [stage(step) for step in range(1, steps + 1)] + [final]


def merge(*streams):
    order = []
    for which, (start, pace, stages) in enumerate(streams):
        for k, stage in enumerate(stages):
            order.append((start + pace * k, which, k, stage))
    for _, _, _, stage in sorted(order, key=lambda item: item[:3]):
        stage()


def kernel(dims, cot, dec, enc, pre, hit, fg_out, ig_out, g0, g1, dv, ev, pv, fg, acc, part, xr, bufs, send, recv, local):
    nx, ny, nz, cut, rcut, width = dims
    hx = nx // 2
    layer = lax.axis_index("layer")
    z = lax.axis_index("feat")
    c = lax.rem(layer, 2)
    y = lax.rem(layer // 2, ny)
    x = layer // (2 * ny)
    is_first = x < hx

    def device(x, y, z, c):
        return ((x * ny + y) * 2 + c, z)

    def shifted(at, n, by):
        return lax.rem(at + by, n)

    sibling = device(x, y, z, 1 - c)
    x_peers = [device(shifted(x, nx, k), y, z, c) for k in range(1, nx)]
    x_right, x_left = x_peers[0], x_peers[-1]
    y_right, y_left = device(x, shifted(y, ny, 1), z, c), device(x, shifted(y, ny, ny - 1), z, c)
    z_right, z_left = device(x, y, shifted(z, nz, 1), c), device(x, y, shifted(z, nz, nz - 1), c)
    peers = [sibling] + x_peers + [y_right, y_left, z_right, z_left]

    own_copies = [
        pltpu.make_async_copy(cot.at[0], g0.at[x, y, z], local.at[0]),
        pltpu.make_async_copy(cot.at[1], g1.at[x, y, z], local.at[1]),
    ]
    for copy in own_copies:
        copy.start()

    barrier = pltpu.get_barrier_semaphore()
    for peer in peers:
        pl.semaphore_signal(barrier, inc=1, device_id=peer, device_id_type=MESH)
    weight_copies = [
        pltpu.make_async_copy(dec.at[1], dv.at[1, c], local.at[2]),
        pltpu.make_async_copy(dec.at[0], dv.at[0, c], local.at[3]),
        pltpu.make_async_copy(enc, ev.at[c], local.at[4]),
        pltpu.make_async_copy(pre.at[:, c], pv.at[c], local.at[5]),
    ]
    for copy in own_copies:
        copy.wait()
    pl.semaphore_wait(barrier, len(peers))

    sems = Semaphores(send, recv)
    drains = []

    lo, hi = pl.ds(0, cut), pl.ds(cut, width - cut)
    rlo, rhi = pl.ds(0, rcut), pl.ds(rcut, width - rcut)
    a_base = sems.take(nx - 1)
    t_base = sems.take(nx - 1)

    def x_copy(k, sent, target):
        at = x if sent else shifted(x, nx, nx - k)
        if target:
            ref = g1.at[at, y, z, :, hi]
            return sems.copy(ref, ref, a_base + k - 1, x_peers[k - 1])
        ref = g0.at[at, y, z]
        return sems.copy(ref, ref, t_base + k - 1, x_peers[k - 1])

    def x_start():
        for k in range(1, nx):
            x_copy(k, True, 1).start()
            pl.when(shifted(x, nx, k) < hx)(lambda k=k: x_copy(k, True, 0).start())

    def x_end():
        for k in range(1, nx):
            x_copy(k, False, 1).wait_recv()

        @pl.when(is_first)
        def _():
            for k in range(1, nx):
                x_copy(k, False, 0).wait_recv()

    def x_drain():
        for k in range(1, nx):
            x_copy(k, True, 1).wait_send()
            pl.when(shifted(x, nx, k) < hx)(lambda k=k: x_copy(k, True, 0).wait_send())

    drains.append(x_drain)

    az = ring_gather(sems, nz, z, z_right, z_left, lambda i, s, r: g1.at[x, y, i, r, lo], 1, drains)
    ay = ring_gather(sems, ny, y, y_right, y_left, lambda i, s, r: g1.at[x, i, :, r, lo], 1, drains)
    ax = ring_gather(sems, nx, x, x_right, x_left, lambda i, s, r: g1.at[i, s, :, r, lo], ny, drains)
    bz = ring_gather(sems, nz, z, z_right, z_left, lambda i, s, r: g1.at[:, y, i, r, hi], 1, drains)
    by = ring_gather(sems, ny, y, y_right, y_left, lambda i, s, r: g1.at[s, i, :, r, hi], nx, drains)
    first_drains = []
    dz = ring_gather(sems, nz, z, z_right, z_left, lambda i, s, r: g0.at[:, y, i, r, rlo], 1, first_drains)
    dy = ring_gather(sems, ny, y, y_right, y_left, lambda i, s, r: g0.at[s, i, :, r, rlo], nx, first_drains)
    cy = ring_gather(sems, ny, y, y_right, y_left, lambda i, s, r: g0.at[:, i, z, r, rhi], 1, first_drains)
    cz = ring_gather(sems, nz, z, z_right, z_left, lambda i, s, r: g0.at[s, :, i, r, rhi], nx, first_drains)

    def joined(*rings):
        stages = list(rings[0])
        for ring in rings[1:]:
            end, start = stages.pop(), ring[0]

            def link(end=end, start=start):
                end()
                start()

            stages.append(link)
            stages.extend(ring[1:])
        return stages

    def first_only(stages):
        def wrap(stage):
            return lambda: pl.when(is_first)(lambda: stage())

        return [wrap(stage) for stage in stages]

    dec1 = sems.copy(dec.at[1], dv.at[1, c], sems.take(), sibling)
    dec0 = sems.copy(dec.at[0], dv.at[0, c], sems.take(), sibling)
    enc1 = sems.copy(enc, ev.at[c], sems.take(), sibling)
    pre1 = sems.copy(pre.at[:, 1 - c], pv.at[c], sems.take(), sibling)

    def weights_start():
        weight_copies[0].start()
        dec1.start()

        @pl.when(is_first)
        def _():
            weight_copies[1].start()
            dec0.start()

        for copy in weight_copies[2:] + [enc1, pre1]:
            copy.start()

    merge(
        (0.0, 1.0, joined(az, ay, ax)),
        (0.1, 1.0, [x_start]),
        (0.2, 1.0, [weights_start]),
        (0.9, 1.0, [x_end]),
        (0.95, 1.0, joined(bz, by)),
        (0.96, 1.0, first_only(joined(dz, dy))),
        (0.97, 1.0, first_only(joined(cy, cz))),
    )

    tokens = nx * ny * ROWS
    feats = dv.shape[2]
    contract = (((1,), (1,)), ((), ()))
    weight_copies[0].wait()
    dec1.wait_recv()

    @pl.when(is_first)
    def _():
        weight_copies[1].wait()
        dec0.wait_recv()

    acc[...] = jnp.zeros_like(acc)

    def act_step(zz, carry):
        columns = pl.ds(pl.multiple_of(zz * width, 128), width)
        rows1 = g1[:, :, zz].reshape(tokens, width)
        for side in range(2):
            acc[side] += lax.dot_general(rows1, dv[1, side, :, columns], contract, preferred_element_type=F32)

        @pl.when(is_first)
        def _():
            rows0 = g0[:, :, zz].reshape(tokens, width)
            for side in range(2):
                acc[side] += lax.dot_general(rows0, dv[0, side, :, columns], contract, preferred_element_type=F32)

        return carry

    lax.fori_loop(0, nz, act_step, 0)
    weight_copies[3].wait()
    pre1.wait_recv()

    def mask_step(w, carry):
        for side in range(2):
            live = (pv[side, w].astype(F32) > 0.0) & (hit[w, :, pl.ds(side * feats, feats)] > 0.0)
            grad = jnp.where(live, acc[side, pl.ds(pl.multiple_of(w * ROWS, ROWS), ROWS), :], 0.0)
            fg[side, w] = grad.astype(BF16)
        return carry

    lax.fori_loop(0, nx * ny, mask_step, 0)
    fg_local = pltpu.make_async_copy(fg.at[c], fg_out.at[:, c], local.at[6])
    fg_index = sems.take()
    fg_remote = sems.copy(fg.at[1 - c], fg_out.at[:, c], fg_index, sibling)
    fg_local.start()
    fg_remote.start()
    weight_copies[2].wait()
    enc1.wait_recv()

    def part_step(zz, carry):
        at = pl.ds(pl.multiple_of(zz * width, 128), width)
        total = None
        for side in range(2):
            term = lax.dot_general(
                fg[side].reshape(tokens, feats), ev[side, at, :], contract, preferred_element_type=F32
            )
            total = term if total is None else total + term
        part[:, :, zz] = total.reshape(nx, ny, ROWS, width)
        return carry

    lax.fori_loop(0, nz, part_step, 0)

    ylo, zhi = pl.ds(0, rcut + 128), pl.ds(rcut + 128, width - rcut - 128)
    y1 = ring_scatter(
        sems, ny, y, y_right, y_left, lambda i, o, j: part.at[o, i, j, :, ylo], nx, nz, bufs[0:4], drains
    )
    z1 = ring_scatter(
        sems, nz, z, z_right, z_left, lambda i, o, j: part.at[o, j, i, :, zhi], nx, ny, bufs[4:8], drains
    )
    z2 = ring_scatter(
        sems, nz, z, z_right, z_left, lambda i, o, j: part.at[o, y, i, :, ylo], nx, 1, bufs[8:12], drains
    )
    y2 = ring_scatter(
        sems, ny, y, y_right, y_left, lambda i, o, j: part.at[o, i, z, :, zhi], nx, 1, bufs[12:16], drains
    )
    merge((0.0, 2.0, joined(y1, z2)), (0.1, 1.0, joined(z1, y2)))

    r_base = sems.take(nx - 1)
    ends = [
        sems.copy(part.at[shifted(x, nx, k), y, z], xr.at[x], r_base + k - 1, x_peers[k - 1]) for k in range(1, nx)
    ]
    for copy in ends:
        copy.start()
    xr[x] = part[x, y, z]
    for k in range(1, nx):
        source = shifted(x, nx, nx - k)
        sems.copy(part.at[source, y, z], xr.at[source], r_base + k - 1, x_peers[k - 1]).wait_recv()
    for source in range(2):
        total = xr[source * hx]
        for k in range(1, hx):
            total = total + xr[source * hx + k]
        ig_out[source] = total.astype(BF16)

    for copy in ends:
        copy.wait_send()
    for drain in drains:
        drain()

    @pl.when(is_first)
    def _():
        for drain in first_drains:
            drain()
        dec0.wait_send()

    for copy in (dec1, enc1, pre1):
        copy.wait_send()
    fg_local.wait()
    fg_remote.wait_send()
    sems.copy(fg.at[c], fg_out.at[:, 1 - c], fg_index, sibling).wait_recv()


def scatter_buffers(n, outer, inner, columns):
    half = (2, outer, inner, HALF, columns)
    full = (max(n // 2 - 1, 1), 2, outer, inner, ROWS, columns)
    return [pltpu.VMEM(half, BF16)] * 2 + [pltpu.VMEM(full, BF16)] * 2


def body(nx, ny, cotangent, decoder, encoder, preact, block_ids, block_counts):
    nz = lax.axis_size("feat")
    num_layers = decoder.shape[1]
    feats, width = decoder.shape[0], cotangent.shape[2]
    windows = preact.shape[0] // WIN
    cut, rcut = width - 128, 256
    groups = nx * ny * 2 // num_layers
    local_blocks = feats // BLOCK
    layer = lax.axis_index("layer")
    source = layer // groups
    chip_layer = layer - layer % 2
    ids = lax.dynamic_index_in_dim(block_ids, source, 0, keepdims=False)
    counts = lax.dynamic_index_in_dim(block_counts, source, 0, keepdims=False)
    slot = (chip_layer % groups + jnp.arange(2)) * nz + lax.axis_index("feat")
    own = (slot[:, None] * local_blocks + jnp.arange(local_blocks)[None, :]).reshape(-1)
    live = jnp.arange(ids.shape[1])[None, :] < counts[:, None]
    found = jnp.any((ids[:, :, None] == own[None, None, :]) & live[:, :, None], axis=1)
    hit = jnp.broadcast_to(found[:, :, None], (windows, 2 * local_blocks, BLOCK)).reshape(windows, 1, 2 * feats)

    any_ref = pl.BlockSpec(memory_space=pl.ANY)
    vmem_ref = pl.BlockSpec(memory_space=pltpu.VMEM)
    tokens = nx * ny * ROWS
    pieces = (nx, ny, nz, ROWS, width)
    ycols = rcut + 128
    bufs = (
        scatter_buffers(ny, nx, nz, ycols)
        + scatter_buffers(nz, nx, ny, width - ycols)
        + scatter_buffers(nz, nx, 1, ycols)
        + scatter_buffers(ny, nx, 1, width - ycols)
    )
    count = 8 * (nx + ny + nz) * max(nx, ny)
    fg, ig = pl.pallas_call(
        functools.partial(kernel, (nx, ny, nz, cut, rcut, width)),
        out_shape=(
            jax.ShapeDtypeStruct((windows, 2, ROWS, feats), BF16),
            jax.ShapeDtypeStruct((num_layers, ROWS, width), BF16),
        ),
        in_specs=[any_ref] * 4 + [vmem_ref],
        out_specs=(any_ref, vmem_ref),
        scratch_shapes=[
            pltpu.VMEM(pieces, BF16),
            pltpu.VMEM(pieces, BF16),
            pltpu.VMEM((num_layers, 2, feats, nz * width), BF16),
            pltpu.VMEM((2, nz * width, feats), BF16),
            pltpu.VMEM((2, windows, ROWS, feats), BF16),
            pltpu.VMEM((2, windows, ROWS, feats), BF16),
            pltpu.VMEM((2, tokens, feats), F32),
            pltpu.VMEM(pieces, F32),
            pltpu.VMEM((nx, ROWS, width), F32),
            bufs,
            pltpu.SemaphoreType.DMA((count,)),
            pltpu.SemaphoreType.DMA((count,)),
            pltpu.SemaphoreType.DMA((7,)),
        ],
        compiler_params=pltpu.CompilerParams(
            collective_id=0, has_side_effects=True, vmem_limit_bytes=60 * 1024 * 1024
        ),
    )(
        cotangent,
        jnp.transpose(decoder, (1, 0, 2)),
        encoder,
        preact.reshape(windows, 2, ROWS, feats),
        hit.astype(F32),
    )
    return fg.reshape(windows * WIN, feats), ig


def solution(mesh, nx=4, ny=4):
    return jax.shard_map(
        functools.partial(body, nx, ny),
        mesh=mesh,
        in_specs=(
            P(None, "layer", "feat"),
            P(("layer", "feat"), None, None),
            P(None, ("layer", "feat")),
            P(None, ("layer", "feat")),
            P(),
            P(),
        ),
        out_specs=(P(None, ("layer", "feat")), P(None, "layer", "feat")),
        check_vma=False,
    )
```

```python
import functools

import jax
import jax.numpy as jnp
from jax import lax
from jax.experimental import pallas as pl
from jax.experimental.pallas import tpu as pltpu
from jax.sharding import PartitionSpec as P

MESH = pl.DeviceIdType.MESH
WIN = 64
ROWS = WIN // 2
HALF = ROWS // 2
BLOCK = 128
F32 = jnp.float32
BF16 = jnp.bfloat16


class Semaphores:
    def __init__(self, send, recv):
        self.send, self.recv, self.used = send, recv, 0

    def take(self, count=1):
        first = self.used
        self.used += count
        return first

    def copy(self, source, target, index, device):
        return pltpu.make_async_remote_copy(
            src_ref=source,
            dst_ref=target,
            send_sem=self.send.at[index],
            recv_sem=self.recv.at[index],
            device_id=device,
            device_id_type=MESH,
        )


def both(index):
    return pl.ds(index * HALF, HALF)


def ring_gather(sems, n, me, right, left, chunk, subs, drains):
    steps = n // 2
    base = sems.take(steps * 2 * subs)
    sides = ((right, -1), (left, 1))

    def copies(step, sub, sent):
        last = step == steps
        found = []
        for side, (device, sign) in enumerate(sides):
            at = lax.rem(me + (n + sign * (step - (1 if sent else 0))), n)
            rows = both(side) if last else pl.ds(0, ROWS)
            ref = chunk(at, sub, rows)
            found.append(sems.copy(ref, ref, base + ((step - 1) * 2 + side) * subs + sub, device))
        return found

    def over(fn):
        if subs == 1:
            fn(0)
        else:
            def loop(sub, carry):
                fn(sub)
                return carry

            lax.fori_loop(0, subs, loop, 0)

    def stage(step):
        def run():
            def one(sub):
                if step > 1:
                    for copy in copies(step - 1, sub, False):
                        copy.wait_recv()
                if step <= steps:
                    for copy in copies(step, sub, True):
                        copy.start()

            over(one)

        return run

    def drain():
        for step in range(1, steps + 1):
            def one(sub):
                for copy in copies(step, sub, True):
                    copy.wait_send()

            over(one)

    drains.append(drain)
    return [stage(step) for step in range(1, steps + 2)]


def ring_scatter(sems, n, me, right, left, own, outer, inner, bufs, drains):
    half_send, half_recv, full_send, full_recv = bufs
    steps = n // 2
    base = sems.take(steps * 2 * outer)
    sides = ((right, 1), (left, -1))

    def copy_of(step, side, o):
        device = sides[side][0]
        index = base + ((step - 1) * 2 + side) * outer + o
        if step == 1:
            return sems.copy(half_send.at[side, o], half_recv.at[side, o], index, device)
        return sems.copy(full_send.at[step - 2, side, o], full_recv.at[step - 2, side, o], index, device)

    def loop_inner(fn):
        if inner == 1:
            fn(0)
        else:
            def loop(j, carry):
                fn(j)
                return carry

            lax.fori_loop(0, inner, loop, 0)

    def stage(step):
        def one(o, carry):
            for side, (_, sign) in enumerate(sides):
                at = lax.rem(me + (n + sign * (steps - step + 1)), n)
                if step > 1:
                    copy_of(step - 1, side, o).wait_recv()

                def add(j):
                    if step == 1:
                        half_send[side, o, j] = own(at, o, j)[pl.ds(side * HALF, HALF), :].astype(BF16)
                    elif step == 2:
                        mine = pl.ds(side * HALF, HALF)
                        other = pl.ds((1 - side) * HALF, HALF)
                        ref = own(at, o, j)
                        full_send[step - 2, side, o, j, mine, :] = (
                            ref[mine, :] + half_recv[side, o, j].astype(F32)
                        ).astype(BF16)
                        full_send[step - 2, side, o, j, other, :] = ref[other, :].astype(BF16)
                    else:
                        full_send[step - 2, side, o, j] = (
                            own(at, o, j)[...] + full_recv[step - 3, side, o, j].astype(F32)
                        ).astype(BF16)

                loop_inner(add)
                copy_of(step, side, o).start()
            return carry

        return lambda: lax.fori_loop(0, outer, one, 0)

    def final():
        def one(o, carry):
            for side in range(2):
                copy_of(steps, side, o).wait_recv()

            def add(j):
                ref = own(me, o, j)
                if steps == 1:
                    for side in range(2):
                        mine = pl.ds(side * HALF, HALF)
                        ref[mine, :] = ref[mine, :] + half_recv[side, o, j].astype(F32)
                else:
                    ref[...] = (
                        ref[...]
                        + full_recv[steps - 2, 0, o, j].astype(F32)
                        + full_recv[steps - 2, 1, o, j].astype(F32)
                    )

            loop_inner(add)
            return carry

        lax.fori_loop(0, outer, one, 0)

    def drain():
        for step in range(1, steps + 1):
            def one(o, carry):
                for side in range(2):
                    copy_of(step, side, o).wait_send()
                return carry

            lax.fori_loop(0, outer, one, 0)

    drains.append(drain)
    return [stage(step) for step in range(1, steps + 1)] + [final]


def merge(*streams):
    order = []
    for which, (start, pace, stages) in enumerate(streams):
        for k, stage in enumerate(stages):
            order.append((start + pace * k, which, k, stage))
    for _, _, _, stage in sorted(order, key=lambda item: item[:3]):
        stage()


class Fan:
    def __init__(self, sems, me, right, left, chunk, parts):
        self.sems, self.me, self.sides, self.chunk, self.parts = sems, me, ((right, 3), (left, 1)), chunk, parts
        self.base = sems.take(4 * parts)

    def copies(self, step, number, part, sent):
        found = []
        for side, (device, by) in enumerate(self.sides):
            at = lax.rem(self.me + by * (step - (1 if sent else 0)), 4)
            ref = self.chunk(at, part, both(side) if step == 2 else pl.ds(0, ROWS))
            index = self.base + (2 * (step - 1) + side) * self.parts + number
            found.append(self.sems.copy(ref, ref, index, device))
        return found

    def first(self, number, part):
        for copy in self.copies(1, number, part, True):
            copy.start()

    def second(self, number, part):
        for copy in self.copies(1, number, part, False):
            copy.wait_recv()
        for copy in self.copies(2, number, part, True):
            copy.start()

    def arrived(self, number, part):
        for copy in self.copies(2, number, part, False):
            copy.wait_recv()

    def sent(self, number, part):
        for step in (1, 2):
            for copy in self.copies(step, number, part, True):
                copy.wait_send()


def kernel(
    dims, cot, dec, enc, pre, ids, counts, fg_out, ig_out, g0, g1, raw, dv, ev, pv, fg, hit, acc, part, xr, bufs, send, recv, local
):
    nx, ny, nz, cut, rcut, width = dims
    hx = nx // 2
    layer = lax.axis_index("layer")
    z = lax.axis_index("feat")
    c = lax.rem(layer, 2)
    y = lax.rem(layer // 2, ny)
    x = layer // (2 * ny)
    is_first = x < hx

    def device(x, y, z, c):
        return ((x * ny + y) * 2 + c, z)

    def shifted(at, n, by):
        return lax.rem(at + by, n)

    sibling = device(x, y, z, 1 - c)
    x_peers = [device(shifted(x, nx, k), y, z, c) for k in range(1, nx)]
    y_peers = [device(x, shifted(y, ny, k), z, c) for k in range(1, ny)]
    x_right, x_left = x_peers[0], x_peers[-1]
    y_right, y_left = y_peers[0], y_peers[-1]
    z_right, z_left = device(x, y, shifted(z, nz, 1), c), device(x, y, shifted(z, nz, nz - 1), c)
    peers = [sibling] + x_peers + y_peers + [z_right, z_left]

    own_copies = [
        pltpu.make_async_copy(cot.at[0], g0.at[x, y, z], local.at[0]),
        pltpu.make_async_copy(cot.at[1], g1.at[x, y, z], local.at[1]),
    ]
    for copy in own_copies:
        copy.start()

    barrier = pltpu.get_barrier_semaphore()
    for peer in peers:
        pl.semaphore_signal(barrier, inc=1, device_id=peer, device_id_type=MESH)
    dec_local = pltpu.make_async_copy(dec, raw, local.at[2])
    enc_local = pltpu.make_async_copy(enc, ev.at[c], local.at[3])
    pre_local = pltpu.make_async_copy(pre.at[:, c], pv.at[c], local.at[4])
    for copy in own_copies:
        copy.wait()
    pl.semaphore_wait(barrier, len(peers))

    sems = Semaphores(send, recv)
    drains = []

    def first_only(stage):
        pl.when(is_first)(lambda: stage())

    lo, hi = pl.ds(0, cut), pl.ds(cut, width - cut)
    rlo, rhi = pl.ds(0, rcut), pl.ds(rcut, width - rcut)

    class Direct:
        def __init__(self, n, me, to, chunk, wanted=None):
            self.n, self.me, self.to, self.chunk, self.wanted = n, me, to, chunk, wanted
            self.base = sems.take(n - 1)

        def copy(self, k, sent):
            ref = self.chunk(self.me if sent else shifted(self.me, self.n, self.n - k))
            return sems.copy(ref, ref, self.base + k - 1, self.to[k - 1])

        def each(self, act):
            for k in range(1, self.n):
                if self.wanted is None:
                    act(k)
                else:
                    pl.when(self.wanted(shifted(self.me, self.n, k)))(lambda k=k: act(k))

        def start(self):
            self.each(lambda k: self.copy(k, True).start())

        def arrived(self):
            for k in range(1, self.n):
                self.copy(k, False).wait_recv()

        def sent(self):
            self.each(lambda k: self.copy(k, True).wait_send())

    ya = Direct(ny, y, y_peers, lambda i: g1.at[x, i, z, :, lo])
    xt = Direct(nx, x, x_peers, lambda i: g0.at[i, y, z], lambda to: to < hx)
    xb = Direct(nx, x, x_peers, lambda i: g1.at[i, y, z, :, hi])
    yc = Direct(ny, y, y_peers, lambda i: g0.at[:, i, z, :, rhi])
    first_drains = []
    za = ring_gather(sems, nz, z, z_right, z_left, lambda i, s, r: g1.at[x, :, i, r, lo], 1, drains)
    zb = ring_gather(sems, nz, z, z_right, z_left, lambda i, s, r: g1.at[:, y, i, r, hi], 1, drains)
    zd = ring_gather(sems, nz, z, z_right, z_left, lambda i, s, r: g0.at[:, y, i, r, rlo], 1, first_drains)
    zc = ring_gather(sems, nz, z, z_right, z_left, lambda i, s, r: g0.at[s, :, i, r, rhi], nx, first_drains)
    xa = Fan(sems, x, x_right, x_left, lambda i, p, r: g1.at[i, :, p, r, lo], nz)
    yb = Fan(sems, y, y_right, y_left, lambda i, p, r: g1.at[:, i, p, r, hi], nz)
    yd = Fan(sems, y, y_right, y_left, lambda i, p, r: g0.at[:, i, p, r, rlo], nz)

    def each_part(step, act):
        if step == 0:
            act(0, z)
        elif step == nz // 2:
            act(nz - 1, shifted(z, nz, nz // 2))
        else:
            def loop(j, carry):
                act(2 * step - 1 + j, lax.rem(z + nz + (2 * j - 1) * step, nz))
                return carry

            lax.fori_loop(0, 2, loop, 0)

    feats = dv.shape[2]
    dec1 = sems.copy(dv.at[1, c], dv.at[1, c], sems.take(), sibling)
    dec0 = sems.copy(dv.at[0, c], dv.at[0, c], sems.take(), sibling)
    enc1 = sems.copy(enc, ev.at[c], sems.take(), sibling)
    pre1 = sems.copy(pre.at[:, 1 - c], pv.at[c], sems.take(), sibling)

    def sort_targets(step):
        def one(j, carry):
            at = pl.multiple_of((step * 4 + j) * 16, 16)
            dv[1, c, pl.ds(at, 16), :] = raw[pl.ds(at, 16)][:, 1, :]

            @pl.when(is_first)
            def _():
                dv[0, c, pl.ds(at, 16), :] = raw[pl.ds(at, 16)][:, 0, :]

            return carry

        lax.fori_loop(0, 4, one, 0)

    ya.start()
    xb.start()
    xt.start()
    for copy in (dec_local, enc_local, pre_local, enc1, pre1):
        copy.start()

    ids_here = ids[layer // (nx * ny)]
    counts_here = jnp.where(is_first, counts[0:1, :], counts[1:2, :]).astype(F32)
    windows = nx * ny
    square = (windows, windows)
    diagonal = lax.broadcasted_iota(jnp.int32, square, 0) == lax.broadcasted_iota(jnp.int32, square, 1)
    column = jnp.sum(jnp.where(diagonal, jnp.broadcast_to(counts_here, square), 0.0), axis=1, keepdims=True)
    live_slots = lax.broadcasted_iota(jnp.int32, ids_here.shape, 1).astype(F32) < column
    blocks = feats // BLOCK
    for side in range(2):
        slot = (lax.rem(layer - c, nx * ny) + side) * nz + z
        for k in range(blocks):
            same = (ids_here == slot * blocks + k) & live_slots
            found = jnp.max(jnp.where(same, 1.0, 0.0), axis=1, keepdims=True)
            hit[side * blocks + k] = jnp.broadcast_to(found, (windows, BLOCK))

    ya.arrived()
    za[0]()
    xb.arrived()
    first_only(xt.arrived)
    zb[0]()
    first_only(zd[0])
    for step in range(nz // 2 + 1):
        if step > 0:
            za[step]()
        each_part(step, xa.first)
        if step > 0:
            zb[step]()
        each_part(step, yb.first)

        def first_step(step=step):
            if step > 0:
                zd[step]()
            each_part(step, yd.first)
            if step == 0:
                yc.start()
            elif step == 1:
                yc.arrived()
            if step > 0:
                zc[step - 1]()

        first_only(first_step)
        if step == 0:
            dec_local.wait()
        if step < nz // 2:
            sort_targets(step)
        if step == nz // 2 - 1:
            dec1.start()
            first_only(dec0.start)
        if step > 0:
            each_part(step - 1, xa.second)
            each_part(step - 1, yb.second)
            first_only(lambda step=step: each_part(step - 1, yd.second))
    each_part(nz // 2, xa.second)
    each_part(nz // 2, yb.second)

    def first_last():
        each_part(nz // 2, yd.second)
        zc[nz // 2]()

    first_only(first_last)

    def numbered(act):
        for step in range(nz // 2 + 1):
            each_part(step, act)

    numbered(xa.arrived)
    numbered(yb.arrived)
    first_only(lambda: numbered(yd.arrived))

    tokens = nx * ny * ROWS
    contract = (((1,), (1,)), ((), ()))
    dec1.wait_recv()
    first_only(dec0.wait_recv)

    acc[...] = jnp.zeros_like(acc)

    def act_step(zz, carry):
        columns = pl.ds(pl.multiple_of(zz * width, 128), width)
        rows1 = g1[:, :, zz].reshape(tokens, width)
        for side in range(2):
            acc[side] += lax.dot_general(rows1, dv[1, side, :, columns], contract, preferred_element_type=F32)

        @pl.when(is_first)
        def _():
            rows0 = g0[:, :, zz].reshape(tokens, width)
            for side in range(2):
                acc[side] += lax.dot_general(rows0, dv[0, side, :, columns], contract, preferred_element_type=F32)

        return carry

    lax.fori_loop(0, nz, act_step, 0)
    pre_local.wait()
    pre1.wait_recv()

    def mask_step(w, carry):
        for side in range(2):
            for k in range(blocks):
                lanes = pl.ds(k * BLOCK, BLOCK)
                live = (pv[side, w, :, lanes].astype(F32) > 0.0) & (hit[side * blocks + k, pl.ds(w, 1), :] > 0.0)
                grad = jnp.where(live, acc[side, pl.ds(pl.multiple_of(w * ROWS, ROWS), ROWS), lanes], 0.0)
                fg[side, w, :, lanes] = grad.astype(BF16)
        return carry

    lax.fori_loop(0, nx * ny, mask_step, 0)
    fg_local = pltpu.make_async_copy(fg.at[c], fg_out.at[:, c], local.at[5])
    fg_index = sems.take()
    fg_remote = sems.copy(fg.at[1 - c], fg_out.at[:, c], fg_index, sibling)
    fg_local.start()
    fg_remote.start()
    enc_local.wait()
    enc1.wait_recv()

    def part_step(zz, carry):
        at = pl.ds(pl.multiple_of(zz * width, 128), width)
        total = None
        for side in range(2):
            term = lax.dot_general(
                fg[side].reshape(tokens, feats), ev[side, at, :], contract, preferred_element_type=F32
            )
            total = term if total is None else total + term
        part[:, :, zz] = total.reshape(nx, ny, ROWS, width)
        return carry

    lax.fori_loop(0, nz, part_step, 0)

    ylo, zhi = pl.ds(0, rcut), pl.ds(rcut, width - rcut)
    def joined(*rings):
        stages = list(rings[0])
        for ring in rings[1:]:
            end, start = stages.pop(), ring[0]

            def link(end=end, start=start):
                end()
                start()

            stages.append(link)
            stages.extend(ring[1:])
        return stages

    y1 = ring_scatter(
        sems, ny, y, y_right, y_left, lambda i, o, j: part.at[o, i, j, :, ylo], nx, nz, bufs[0:4], drains
    )
    z1 = ring_scatter(
        sems, nz, z, z_right, z_left, lambda i, o, j: part.at[o, j, i, :, zhi], nx, ny, bufs[4:8], drains
    )
    z2 = ring_scatter(
        sems, nz, z, z_right, z_left, lambda i, o, j: part.at[o, y, i, :, ylo], nx, 1, bufs[8:12], drains
    )
    y2 = ring_scatter(
        sems, ny, y, y_right, y_left, lambda i, o, j: part.at[o, i, z, :, zhi], nx, 1, bufs[12:16], drains
    )
    merge((0.0, 2.0, joined(y1, z2)), (0.1, 1.0, joined(z1, y2)))

    r_base = sems.take(nx - 1)
    ends = [
        sems.copy(part.at[shifted(x, nx, k), y, z], xr.at[x], r_base + k - 1, x_peers[k - 1]) for k in range(1, nx)
    ]
    for copy in ends:
        copy.start()
    xr[x] = part[x, y, z]
    for k in range(1, nx):
        source = shifted(x, nx, nx - k)
        sems.copy(part.at[source, y, z], xr.at[source], r_base + k - 1, x_peers[k - 1]).wait_recv()
    for source in range(2):
        total = xr[source * hx]
        for k in range(1, hx):
            total = total + xr[source * hx + k]
        ig_out[source] = total.astype(BF16)

    for copy in ends:
        copy.wait_send()
    for drain in drains:
        drain()

    for direct in (ya, xb, xt):
        direct.sent()
    numbered(xa.sent)
    numbered(yb.sent)

    def first_sent():
        for drain in first_drains:
            drain()
        yc.sent()
        numbered(yd.sent)
        dec0.wait_send()

    first_only(first_sent)
    for copy in (dec1, enc1, pre1):
        copy.wait_send()
    fg_local.wait()
    fg_remote.wait_send()
    sems.copy(fg.at[c], fg_out.at[:, 1 - c], fg_index, sibling).wait_recv()


def scatter_buffers(n, outer, inner, columns):
    half = (2, outer, inner, HALF, columns)
    full = (max(n // 2 - 1, 1), 2, outer, inner, ROWS, columns)
    return [pltpu.VMEM(half, BF16)] * 2 + [pltpu.VMEM(full, BF16)] * 2


def body(nx, ny, cotangent, decoder, encoder, preact, block_ids, block_counts):
    nz = lax.axis_size("feat")
    num_layers = decoder.shape[1]
    feats, width = decoder.shape[0], cotangent.shape[2]
    windows = preact.shape[0] // WIN
    cut, rcut = width - 128, width - 256
    any_ref = pl.BlockSpec(memory_space=pl.ANY)
    vmem_ref = pl.BlockSpec(memory_space=pltpu.VMEM)
    tokens = nx * ny * ROWS
    pieces = (nx, ny, nz, ROWS, width)
    ycols = rcut
    bufs = (
        scatter_buffers(ny, nx, nz, ycols)
        + scatter_buffers(nz, nx, ny, width - ycols)
        + scatter_buffers(nz, nx, 1, ycols)
        + scatter_buffers(ny, nx, 1, width - ycols)
    )
    count = 8 * (nx + ny + nz) * max(nx, ny)
    fg, ig = pl.pallas_call(
        functools.partial(kernel, (nx, ny, nz, cut, rcut, width)),
        out_shape=(
            jax.ShapeDtypeStruct((windows, 2, ROWS, feats), BF16),
            jax.ShapeDtypeStruct((num_layers, ROWS, width), BF16),
        ),
        in_specs=[any_ref] * 4 + [vmem_ref] * 2,
        out_specs=(any_ref, vmem_ref),
        scratch_shapes=[
            pltpu.VMEM(pieces, BF16),
            pltpu.VMEM(pieces, BF16),
            pltpu.VMEM((feats, num_layers, nz * width), BF16),
            pltpu.VMEM((num_layers, 2, feats, nz * width), BF16),
            pltpu.VMEM((2, nz * width, feats), BF16),
            pltpu.VMEM((2, windows, ROWS, feats), BF16),
            pltpu.VMEM((2, windows, ROWS, feats), BF16),
            pltpu.VMEM((2 * feats // BLOCK, windows, BLOCK), F32),
            pltpu.VMEM((2, tokens, feats), F32),
            pltpu.VMEM(pieces, F32),
            pltpu.VMEM((nx, ROWS, width), F32),
            bufs,
            pltpu.SemaphoreType.DMA((count,)),
            pltpu.SemaphoreType.DMA((count,)),
            pltpu.SemaphoreType.DMA((7,)),
        ],
        compiler_params=pltpu.CompilerParams(
            collective_id=0, has_side_effects=True, vmem_limit_bytes=60 * 1024 * 1024
        ),
    )(
        cotangent,
        decoder,
        encoder,
        preact.reshape(windows, 2, ROWS, feats),
        block_ids,
        block_counts,
    )
    return fg.reshape(windows * WIN, feats), ig


def solution(mesh, nx=4, ny=4):
    return jax.shard_map(
        functools.partial(body, nx, ny),
        mesh=mesh,
        in_specs=(
            P(None, "layer", "feat"),
            P(("layer", "feat"), None, None),
            P(None, ("layer", "feat")),
            P(None, ("layer", "feat")),
            P(),
            P(),
        ),
        out_specs=(P(None, ("layer", "feat")), P(None, "layer", "feat")),
        check_vma=False,
    )
```

```python
import functools

import jax
import jax.numpy as jnp
from jax import lax
from jax.experimental import pallas as pl
from jax.experimental.pallas import tpu as pltpu
from jax.sharding import PartitionSpec as P

MESH = pl.DeviceIdType.MESH
WIN = 64
ROWS = WIN // 2
WAVES = 2
STRIP = ROWS // WAVES
BLOCK = 128
SIDE = 4
F32 = jnp.float32
BF16 = jnp.bfloat16
WHOLE = pl.ds(0, SIDE)
CONTRACT = (((1,), (1,)), ((), ()))


def half(side):
    return pl.ds(side * (SIDE // 2), SIDE // 2)


def repeat(count, fn):
    if count == 1:
        fn(0)
        return

    def loop(i, carry):
        fn(i)
        return carry

    lax.fori_loop(0, count, loop, 0)


class Semaphores:
    def __init__(self, send, recv):
        self.send, self.recv, self.used = send, recv, 0

    def take(self, count=1):
        first = self.used
        self.used += count
        return first

    def copy(self, source, target, index, device):
        return pltpu.make_async_remote_copy(
            src_ref=source,
            dst_ref=target,
            send_sem=self.send.at[index],
            recv_sem=self.recv.at[index],
            device_id=device,
            device_id_type=MESH,
        )


class Direct:
    def __init__(self, sems, n, me, to, chunk, wanted=None):
        self.sems, self.n, self.me, self.to, self.chunk, self.wanted = sems, n, me, to, chunk, wanted
        self.base = sems.take(n - 1)

    def copy(self, k, sent):
        ref = self.chunk(self.me if sent else lax.rem(self.me + self.n - k, self.n))
        return self.sems.copy(ref, ref, self.base + k - 1, self.to[k - 1])

    def each(self, act):
        for k in range(1, self.n):
            if self.wanted is None:
                act(k)
            else:
                pl.when(self.wanted(lax.rem(self.me + k, self.n)))(lambda k=k: act(k))

    def start(self):
        self.each(lambda k: self.copy(k, True).start())

    def arrived(self):
        for k in range(1, self.n):
            self.copy(k, False).wait_recv()

    def sent(self):
        self.each(lambda k: self.copy(k, True).wait_send())


class Ring:
    def __init__(self, sems, n, me, right, left, chunk, parts):
        self.sems, self.n, self.me, self.sides = sems, n, me, ((right, -1), (left, 1))
        self.chunk, self.parts, self.steps = chunk, parts, n // 2
        self.base = sems.take(2 * self.steps * parts)

    def copies(self, step, number, part, sent):
        found = []
        for side, (device, sign) in enumerate(self.sides):
            at = lax.rem(self.me + self.n + sign * (step - (1 if sent else 0)), self.n)
            ref = self.chunk(at, part, half(side) if step == self.steps else WHOLE)
            index = self.base + (2 * (step - 1) + side) * self.parts + number
            found.append(self.sems.copy(ref, ref, index, device))
        return found

    def step(self, step, number=0, part=0):
        if step > 1:
            for copy in self.copies(step - 1, number, part, False):
                copy.wait_recv()
        if step <= self.steps:
            for copy in self.copies(step, number, part, True):
                copy.start()

    def sent(self, number=0, part=0):
        for step in range(1, self.steps + 1):
            for copy in self.copies(step, number, part, True):
                copy.wait_send()


class Scatter:
    def __init__(self, sems, n, me, right, left, own, outer, inner, columns, bufs):
        self.half_send, self.half_recv, self.full_send, self.full_recv = bufs
        self.sems, self.n, self.me, self.own, self.outer, self.inner = sems, n, me, own, outer, inner
        self.columns, self.steps = columns, n // 2
        self.sides = ((right, 1), (left, -1))
        self.base = sems.take(2 * self.steps * outer)

    def copy(self, step, side, o):
        index = self.base + ((step - 1) * 2 + side) * self.outer + o
        device = self.sides[side][0]
        if step == 1:
            return self.sems.copy(self.half_send.at[side, o], self.half_recv.at[side, o], index, device)
        return self.sems.copy(self.full_send.at[step - 2, side, o], self.full_recv.at[step - 2, side, o], index, device)

    def fill(self, step, side, o, at):
        own, count = self.own, self.inner // 2
        lanes = pl.ds(side * (self.columns // 2), self.columns // 2)
        others = pl.ds((1 - side) * (self.columns // 2), self.columns // 2)
        if step == 1 and self.inner == 1:
            self.half_send[side, o, 0] = own(at, o, 0)[:, lanes].astype(BF16)
        elif step == 1:
            def one(j):
                self.half_send[side, o, j] = own(at, o, side * count + j)[...].astype(BF16)

            repeat(count, one)
        elif step == 2 and self.inner == 1:
            ref = own(at, o, 0)
            self.full_send[0, side, o, 0, :, lanes] = (
                ref[:, lanes] + self.half_recv[side, o, 0].astype(F32)
            ).astype(BF16)
            self.full_send[0, side, o, 0, :, others] = ref[:, others].astype(BF16)
        elif step == 2:
            def one(j):
                mine, other = side * count + j, (1 - side) * count + j
                self.full_send[0, side, o, mine] = (
                    own(at, o, mine)[...] + self.half_recv[side, o, j].astype(F32)
                ).astype(BF16)
                self.full_send[0, side, o, other] = own(at, o, other)[...].astype(BF16)

            repeat(count, one)
        else:
            def one(j):
                self.full_send[step - 2, side, o, j] = (
                    own(at, o, j)[...] + self.full_recv[step - 3, side, o, j].astype(F32)
                ).astype(BF16)

            repeat(self.inner, one)

    def step(self, step, o):
        for side, (_, sign) in enumerate(self.sides):
            if step > 1:
                self.copy(step - 1, side, o).wait_recv()
            self.fill(step, side, o, lax.rem(self.me + self.n + sign * (self.steps - step + 1), self.n))
            self.copy(step, side, o).start()

    def final(self, o):
        for side in range(2):
            self.copy(self.steps, side, o).wait_recv()

        def add(j):
            ref = self.own(self.me, o, j)
            last = self.steps - 2
            ref[...] = ref[...] + self.full_recv[last, 0, o, j].astype(F32) + self.full_recv[last, 1, o, j].astype(F32)

        repeat(self.inner, add)

    def sent(self, o):
        for step in range(1, self.steps + 1):
            for side in range(2):
                self.copy(step, side, o).wait_send()


def kernel(
    dims, cot, dec, enc, pre, ids, counts, fg_out, ig_out, g0, g1, raw, dv, ev, pv, fg, hit, acc, part, xr, bufs, send, recv, local
):
    nx, ny, nz, rcut, ycut, width = dims
    hx = nx // 2
    windows, feats = nx * ny, dv.shape[2]
    layer = lax.axis_index("layer")
    z = lax.axis_index("feat")
    c = lax.rem(layer, 2)
    y = lax.rem(layer // 2, ny)
    x = layer // (2 * ny)
    is_first = x < hx

    def device(x, y, z, c):
        return ((x * ny + y) * 2 + c, z)

    def shifted(at, n, by):
        return lax.rem(at + by, n)

    def first_only(act):
        pl.when(is_first)(lambda: act())

    sibling = device(x, y, z, 1 - c)
    x_peers = [device(shifted(x, nx, k), y, z, c) for k in range(1, nx)]
    y_peers = [device(x, shifted(y, ny, k), z, c) for k in range(1, ny)]
    z_peers = [device(x, y, shifted(z, nz, k), c) for k in range(1, nz)]
    x_sides, y_sides, z_sides = [(to[0], to[-1]) for to in (x_peers, y_peers, z_peers)]
    peers = [sibling] + x_peers + y_peers + z_peers

    own_copies = [
        pltpu.make_async_copy(cot.at[0], g0.at[x, y, z], local.at[0]),
        pltpu.make_async_copy(cot.at[1], g1.at[x, y, z], local.at[1]),
    ]
    for copy in own_copies:
        copy.start()
    barrier = pltpu.get_barrier_semaphore()
    for peer in peers:
        pl.semaphore_signal(barrier, inc=1, device_id=peer, device_id_type=MESH)
    dec_local = pltpu.make_async_copy(dec, raw, local.at[2])
    enc_local = pltpu.make_async_copy(enc, ev.at[c], local.at[3])
    pre_local = pltpu.make_async_copy(pre.at[:, c], pv.at[c], local.at[4])
    for copy in own_copies:
        copy.wait()
    pl.semaphore_wait(barrier, len(peers))

    sems = Semaphores(send, recv)
    rlo, rhi = pl.ds(0, rcut), pl.ds(rcut, width - rcut)
    ylo, zhi = pl.ds(0, ycut), pl.ds(ycut, width - ycut)

    dec1 = sems.copy(dv.at[1, c], dv.at[1, c], sems.take(), sibling)
    dec0 = sems.copy(dv.at[0, c], dv.at[0, c], sems.take(), sibling)
    enc1 = sems.copy(enc, ev.at[c], sems.take(), sibling)
    pre1 = sems.copy(pre.at[:, 1 - c], pv.at[c], sems.take(), sibling)

    def sort_targets(quarter):
        def one(j):
            at = pl.multiple_of((quarter * (feats // 64) + j) * 16, 16)
            dv[1, c, pl.ds(at, 16), :] = raw[pl.ds(at, 16)][:, 1, :]

            @pl.when(is_first)
            def _():
                dv[0, c, pl.ds(at, 16), :] = raw[pl.ds(at, 16)][:, 0, :]

        repeat(feats // 64, one)

    def each_part(step, act):
        if step == 0:
            act(0, z)
        elif step == nz // 2:
            act(nz - 1, shifted(z, nz, nz // 2))
        else:
            repeat(2, lambda j: act(2 * step - 1 + j, lax.rem(z + nz + (2 * j - 1) * step, nz)))

    def all_parts(act):
        for step in range(nz // 2 + 1):
            each_part(step, act)

    def find_blocks():
        ids_here = ids[layer // windows]
        counts_here = jnp.where(is_first, counts[0:1, :], counts[1:2, :]).astype(F32)
        square = (windows, windows)
        diagonal = lax.broadcasted_iota(jnp.int32, square, 0) == lax.broadcasted_iota(jnp.int32, square, 1)
        column = jnp.sum(jnp.where(diagonal, jnp.broadcast_to(counts_here, square), 0.0), axis=1, keepdims=True)
        live_slots = lax.broadcasted_iota(jnp.int32, ids_here.shape, 1).astype(F32) < column
        for side in range(2):
            slot = (lax.rem(layer - c, windows) + side) * nz + z
            for k in range(feats // BLOCK):
                same = (ids_here == slot * (feats // BLOCK) + k) & live_slots
                found = jnp.max(jnp.where(same, 1.0, 0.0), axis=1, keepdims=True)
                hit[side * (feats // BLOCK) + k] = jnp.broadcast_to(found, (windows, BLOCK))

    class Wave:
        def __init__(self, wave):
            rows = pl.ds(wave * STRIP, STRIP)
            self.wave, self.rows = wave, rows
            self.ya = Direct(sems, ny, y, y_peers, lambda i: g1.at[x, i, z, rows, :])
            self.xt = Direct(sems, nx, x, x_peers, lambda i: g0.at[i, y, z, rows, :], lambda to: to < hx)
            self.yc = Direct(sems, ny, y, y_peers, lambda i: g0.at[:, i, z, rows, rhi])
            self.za = Ring(sems, nz, z, *z_sides, lambda i, p, h: g1.at[x, h, i, rows, :], 1)
            self.zd = Ring(sems, nz, z, *z_sides, lambda i, p, h: g0.at[h, y, i, rows, rlo], 1)
            self.zc = Ring(sems, nz, z, *z_sides, lambda i, p, h: g0.at[p, h, i, rows, rhi], nx)
            self.xa = Ring(sems, nx, x, *x_sides, lambda i, p, h: g1.at[i, h, p, rows, :], nz)
            self.yd = Ring(sems, ny, y, *y_sides, lambda i, p, h: g0.at[h, i, p, rows, rlo], nz)
            own = bufs[wave]
            self.y1 = Scatter(
                sems, ny, y, *y_sides, lambda i, o, j: part.at[o, i, j, rows, ylo], nx, nz, ycut, own[0:4]
            )
            self.z1 = Scatter(
                sems, nz, z, *z_sides, lambda i, o, j: part.at[o, j, i, rows, zhi], nx, ny, width - ycut, own[4:8]
            )
            self.y2 = Scatter(
                sems, ny, y, *y_sides, lambda i, o, j: part.at[o, i, z, rows, zhi], nx, 1, width - ycut, own[8:12]
            )
            self.z_send, self.z_recv = own[12:14]
            self.z2_base = sems.take(nx * nz)
            self.end_base = sems.take(nx)
            self.fg_base = sems.take()

        def begin(self):
            self.ya.start()
            self.xt.start()

        def gather(self, step):
            if step == 0:
                self.ya.arrived()
            self.za.step(step + 1)
            each_part(step, lambda n, p: self.xa.step(1, n, p))

            def first():
                if step == 0:
                    self.xt.arrived()
                self.zd.step(step + 1)
                each_part(step, lambda n, p: self.yd.step(1, n, p))
                if step == 0:
                    self.yc.start()
                elif step == 1:
                    self.yc.arrived()
                if step > 0:
                    repeat(nx, lambda s: self.zc.step(step, s, s))

            first_only(first)
            if step > 0:
                each_part(step - 1, lambda n, p: self.xa.step(2, n, p))
                first_only(lambda: each_part(step - 1, lambda n, p: self.yd.step(2, n, p)))

        def gather_last(self):
            each_part(nz // 2, lambda n, p: self.xa.step(2, n, p))

            def first():
                each_part(nz // 2, lambda n, p: self.yd.step(2, n, p))
                repeat(nx, lambda s: self.zc.step(nz // 2 + 1, s, s))

            first_only(first)

        def gathered(self):
            all_parts(lambda n, p: self.xa.step(3, n, p))
            first_only(lambda: all_parts(lambda n, p: self.yd.step(3, n, p)))

        def act(self):
            tokens = windows * STRIP

            def one(zz):
                columns = pl.ds(pl.multiple_of(zz * width, 128), width)
                rows1 = g1[:, :, zz, self.rows, :].reshape(tokens, width)
                for side in range(2):
                    term = lax.dot_general(rows1, dv[1, side, :, columns], CONTRACT, preferred_element_type=F32)
                    acc[side] += term

                @pl.when(is_first)
                def _():
                    rows0 = g0[:, :, zz, self.rows, :].reshape(tokens, width)
                    for side in range(2):
                        term = lax.dot_general(rows0, dv[0, side, :, columns], CONTRACT, preferred_element_type=F32)
                        acc[side] += term

            acc[...] = jnp.zeros_like(acc)
            repeat(nz, one)

        def mask(self):
            def one(w):
                at = pl.ds(pl.multiple_of(w * STRIP, STRIP), STRIP)
                for side in range(2):
                    for k in range(feats // BLOCK):
                        lanes = pl.ds(k * BLOCK, BLOCK)
                        found = hit[side * (feats // BLOCK) + k, pl.ds(w, 1), :] > 0.0
                        live = (pv[side, w, self.rows, lanes].astype(F32) > 0.0) & found
                        fg[side, w, self.rows, lanes] = jnp.where(live, acc[side, at, lanes], 0.0).astype(BF16)

            repeat(windows, one)
            self.fg_copy("local").start()
            self.fg_copy("sent").start()

        def fg_copy(self, which):
            rows = self.rows
            if which == "local":
                return pltpu.make_async_copy(fg.at[c, :, rows], fg_out.at[:, c, rows], local.at[5 + self.wave])
            to = c if which == "sent" else 1 - c
            return sems.copy(fg.at[1 - c, :, rows], fg_out.at[:, to, rows], self.fg_base, sibling)

        def partial(self):
            def one(zz):
                at = pl.ds(pl.multiple_of(zz * width, 128), width)
                total = None
                for side in range(2):
                    grads = fg[side, :, self.rows, :].reshape(windows * STRIP, feats)
                    term = lax.dot_general(grads, ev[side, at, :], CONTRACT, preferred_element_type=F32)
                    total = term if total is None else total + term
                part[:, :, zz, self.rows, :] = total.reshape(nx, ny, STRIP, width)

            repeat(nz, one)

        def z2_copy(self, o, k, sent):
            at = lax.rem(z + k, nz) if sent else lax.rem(z + nz - k, nz)
            index = self.z2_base + o * nz + k
            to = (layer, lax.rem(z + k, nz))
            if sent:
                return sems.copy(self.z_send.at[o, at], self.z_recv.at[o, z], index, to)
            return sems.copy(self.z_send.at[o, at], self.z_recv.at[o, at], index, to)

        def z2_start(self, o):
            def one(k):
                at = lax.rem(z + k + 1, nz)
                self.z_send[o, at] = part[o, y, at, self.rows, ylo].astype(BF16)
                self.z2_copy(o, k + 1, True).start()

            repeat(nz - 1, one)

        def z2_final(self, o):
            total = part[o, y, z, self.rows, ylo]
            for k in range(1, nz):
                self.z2_copy(o, k, False).wait_recv()
            for k in range(1, nz):
                total = total + self.z_recv[o, lax.rem(z + nz - k, nz)].astype(F32)
            part[o, y, z, self.rows, ylo] = total

        def reduce(self, stage):
            steps = nz // 2
            if stage == 1:
                repeat(nx, lambda o: self.y1.step(1, o))
                repeat(nx, lambda o: self.z1.step(1, o))
            elif stage == 2:
                repeat(nx, lambda o: self.y1.step(2, o))
                repeat(nx, lambda o: self.z1.step(2, o))
            elif stage == 3:
                repeat(nx, lambda o: self.z1.step(3, o))
            elif stage == 4:
                def one(o):
                    self.y1.final(o)
                    self.z2_start(o)

                repeat(nx, one)
            elif stage == 5:
                repeat(nx, lambda o: self.z1.step(4, o))
            elif stage == 6:
                def one(o):
                    self.z1.final(o)
                    self.y2.step(1, o)

                repeat(nx, one)
            elif stage == 7:
                repeat(nx, lambda o: self.y2.step(2, o))
                repeat(nx, self.z2_final)
            elif stage == 8:
                repeat(nx, self.y2.final)
                for k in range(1, nx):
                    self.end_copy(k, True).start()
                xr[x, self.rows] = part[x, y, z, self.rows, :]

        def end_copy(self, k, sent):
            if sent:
                to = shifted(x, nx, k)
                source, target = part.at[to, y, z, self.rows], xr.at[x, self.rows]
            else:
                at = shifted(x, nx, nx - k)
                source, target = part.at[at, y, z, self.rows], xr.at[at, self.rows]
            return sems.copy(source, target, self.end_base + k, x_peers[k - 1])

        def finish(self):
            for k in range(1, nx):
                self.end_copy(k, False).wait_recv()
            for source in range(2):
                total = xr[source * hx, self.rows]
                for k in range(1, hx):
                    total = total + xr[source * hx + k, self.rows]
                ig_out[source, self.rows] = total.astype(BF16)

        def drain(self):
            self.ya.sent()
            self.xt.sent()
            self.za.sent()
            all_parts(self.xa.sent)

            def first():
                self.yc.sent()
                self.zd.sent()
                repeat(nx, lambda s: self.zc.sent(s, s))
                all_parts(self.yd.sent)

            first_only(first)

            def one(o):
                self.y1.sent(o)
                self.z1.sent(o)
                self.y2.sent(o)
                repeat(nz - 1, lambda k: self.z2_copy(o, k + 1, True).wait_send())

            repeat(nx, one)
            for k in range(1, nx):
                self.end_copy(k, True).wait_send()
            self.fg_copy("local").wait()
            self.fg_copy("sent").wait_send()
            self.fg_copy("arrived").wait_recv()

    one, two = Wave(0), Wave(1)
    one.begin()
    for copy in (dec_local, enc_local, pre_local, enc1, pre1):
        copy.start()
    find_blocks()
    one.gather(0)
    dec_local.wait()
    sort_targets(0)
    one.gather(1)
    sort_targets(1)
    one.gather(2)
    two.begin()
    sort_targets(2)
    one.gather(3)
    two.gather(0)
    sort_targets(3)
    dec1.start()
    first_only(dec0.start)
    one.gather(4)
    two.gather(1)
    one.gather_last()
    two.gather(2)
    dec1.wait_recv()
    first_only(dec0.wait_recv)
    pre_local.wait()
    pre1.wait_recv()
    enc_local.wait()
    enc1.wait_recv()
    one.gathered()
    one.act()
    two.gather(3)
    one.mask()
    one.partial()
    one.reduce(1)
    two.gather(4)
    one.reduce(2)
    two.gather_last()
    one.reduce(3)
    one.reduce(4)
    one.reduce(5)
    two.gathered()
    two.act()
    two.mask()
    one.reduce(6)
    two.partial()
    two.reduce(1)
    one.reduce(7)
    two.reduce(2)
    one.reduce(8)
    two.reduce(3)
    two.reduce(4)
    two.reduce(5)
    one.finish()
    two.reduce(6)
    two.reduce(7)
    two.reduce(8)
    one.drain()
    two.finish()
    two.drain()
    for copy in (dec1, enc1, pre1):
        copy.wait_send()
    first_only(dec0.wait_send)


def scatter_buffers(n, outer, inner, columns):
    few = (2, outer, inner // 2, STRIP, columns) if inner > 1 else (2, outer, 1, STRIP, columns // 2)
    full = (n // 2 - 1, 2, outer, inner, STRIP, columns)
    return [pltpu.VMEM(few, BF16)] * 2 + [pltpu.VMEM(full, BF16)] * 2


def body(cotangent, decoder, encoder, preact, block_ids, block_counts):
    nx = ny = SIDE
    nz = lax.axis_size("feat")
    num_layers = decoder.shape[1]
    feats, width = decoder.shape[0], cotangent.shape[2]
    windows = preact.shape[0] // WIN
    rcut, ycut = width - 128, width - 256
    any_ref = pl.BlockSpec(memory_space=pl.ANY)
    vmem_ref = pl.BlockSpec(memory_space=pltpu.VMEM)
    pieces = (nx, ny, nz, ROWS, width)
    bufs = [
        scatter_buffers(ny, nx, nz, ycut)
        + scatter_buffers(nz, nx, ny, width - ycut)
        + scatter_buffers(ny, nx, 1, width - ycut)
        + [pltpu.VMEM((nx, nz, STRIP, ycut), BF16)] * 2
    ] * WAVES
    fg, ig = pl.pallas_call(
        functools.partial(kernel, (nx, ny, nz, rcut, ycut, width)),
        out_shape=(
            jax.ShapeDtypeStruct((windows, 2, ROWS, feats), BF16),
            jax.ShapeDtypeStruct((num_layers, ROWS, width), BF16),
        ),
        in_specs=[any_ref] * 4 + [vmem_ref] * 2,
        out_specs=(any_ref, vmem_ref),
        scratch_shapes=[
            pltpu.VMEM(pieces, BF16),
            pltpu.VMEM(pieces, BF16),
            pltpu.VMEM((feats, num_layers, nz * width), BF16),
            pltpu.VMEM((num_layers, 2, feats, nz * width), BF16),
            pltpu.VMEM((2, nz * width, feats), BF16),
            pltpu.VMEM((2, windows, ROWS, feats), BF16),
            pltpu.VMEM((2, windows, ROWS, feats), BF16),
            pltpu.VMEM((2 * feats // BLOCK, windows, BLOCK), F32),
            pltpu.VMEM((2, windows * STRIP, feats), F32),
            pltpu.VMEM(pieces, F32),
            pltpu.VMEM((nx, ROWS, width), F32),
            bufs,
            pltpu.SemaphoreType.DMA((512,)),
            pltpu.SemaphoreType.DMA((512,)),
            pltpu.SemaphoreType.DMA((5 + WAVES,)),
        ],
        compiler_params=pltpu.CompilerParams(
            collective_id=0, has_side_effects=True, vmem_limit_bytes=60 * 1024 * 1024
        ),
    )(cotangent, decoder, encoder, preact.reshape(windows, 2, ROWS, feats), block_ids, block_counts)
    return fg.reshape(windows * WIN, feats), ig


def solution(mesh):
    return jax.shard_map(
        body,
        mesh=mesh,
        in_specs=(
            P(None, "layer", "feat"),
            P(("layer", "feat"), None, None),
            P(None, ("layer", "feat")),
            P(None, ("layer", "feat")),
            P(),
            P(),
        ),
        out_specs=(P(None, ("layer", "feat")), P(None, "layer", "feat")),
        check_vma=False,
    )
```

```python
import functools

import jax
import jax.numpy as jnp
from jax import lax
from jax.experimental import pallas as pl
from jax.experimental.pallas import tpu as pltpu
from jax.sharding import PartitionSpec as P

MESH = pl.DeviceIdType.MESH
WIN = 64
ROWS = WIN // 2
WAVES = 2
STRIP = ROWS // WAVES
BLOCK = 128
SIDE = 4
F32 = jnp.float32
BF16 = jnp.bfloat16
WHOLE = pl.ds(0, SIDE)
CONTRACT = (((1,), (1,)), ((), ()))


def half(side):
    return pl.ds(side * (SIDE // 2), SIDE // 2)


def repeat(count, fn):
    if count == 1:
        fn(0)
        return

    def loop(i, carry):
        fn(i)
        return carry

    lax.fori_loop(0, count, loop, 0)


class Semaphores:
    def __init__(self, send, recv):
        self.send, self.recv, self.used = send, recv, 0

    def take(self, count=1):
        first = self.used
        self.used += count
        return first

    def copy(self, source, target, index, device):
        return pltpu.make_async_remote_copy(
            src_ref=source,
            dst_ref=target,
            send_sem=self.send.at[index],
            recv_sem=self.recv.at[index],
            device_id=device,
            device_id_type=MESH,
        )


class Direct:
    def __init__(self, sems, n, me, to, chunk, wanted=None):
        self.sems, self.n, self.me, self.to, self.chunk, self.wanted = sems, n, me, to, chunk, wanted
        self.base = sems.take(n - 1)

    def copy(self, k, sent):
        ref = self.chunk(self.me if sent else lax.rem(self.me + self.n - k, self.n))
        return self.sems.copy(ref, ref, self.base + k - 1, self.to[k - 1])

    def each(self, act):
        for k in range(1, self.n):
            if self.wanted is None:
                act(k)
            else:
                pl.when(self.wanted(lax.rem(self.me + k, self.n)))(lambda k=k: act(k))

    def start(self):
        self.each(lambda k: self.copy(k, True).start())

    def arrived(self):
        for k in range(1, self.n):
            self.copy(k, False).wait_recv()

    def sent(self):
        self.each(lambda k: self.copy(k, True).wait_send())


class Ring:
    def __init__(self, sems, n, me, right, left, chunk, parts):
        self.sems, self.n, self.me, self.sides = sems, n, me, ((right, -1), (left, 1))
        self.chunk, self.parts, self.steps = chunk, parts, n // 2
        self.base = sems.take(2 * self.steps * parts)

    def copies(self, step, number, part, sent):
        found = []
        for side, (device, sign) in enumerate(self.sides):
            at = lax.rem(self.me + self.n + sign * (step - (1 if sent else 0)), self.n)
            ref = self.chunk(at, part, half(side) if step == self.steps else WHOLE)
            index = self.base + (2 * (step - 1) + side) * self.parts + number
            found.append(self.sems.copy(ref, ref, index, device))
        return found

    def step(self, step, number=0, part=0):
        if step > 1:
            for copy in self.copies(step - 1, number, part, False):
                copy.wait_recv()
        if step <= self.steps:
            for copy in self.copies(step, number, part, True):
                copy.start()

    def sent(self, number=0, part=0):
        for step in range(1, self.steps + 1):
            for copy in self.copies(step, number, part, True):
                copy.wait_send()


class Scatter:
    def __init__(self, sems, n, me, right, left, own, outer, inner, bufs):
        self.half_send, self.half_recv, self.full_send, self.full_recv = bufs
        self.sems, self.n, self.me, self.own, self.outer, self.inner = sems, n, me, own, outer, inner
        self.steps = n // 2
        self.sides = ((right, 1), (left, -1))
        self.base = sems.take(2 * self.steps * outer)

    def copy(self, step, side, o):
        index = self.base + ((step - 1) * 2 + side) * self.outer + o
        device = self.sides[side][0]
        if step == 1:
            return self.sems.copy(self.half_send.at[side, o], self.half_recv.at[side, o], index, device)
        return self.sems.copy(self.full_send.at[step - 2, side, o], self.full_recv.at[step - 2, side, o], index, device)

    def fill(self, step, side, o, at):
        count = self.inner // 2
        mine, others = pl.ds(side * count, count), pl.ds((1 - side) * count, count)
        if step == 1:
            self.half_send[side, o] = self.own(at, o, mine)[...].astype(BF16)
        elif step == 2:
            self.full_send[0, side, o, mine] = (
                self.own(at, o, mine)[...] + self.half_recv[side, o].astype(F32)
            ).astype(BF16)
            self.full_send[0, side, o, others] = self.own(at, o, others)[...].astype(BF16)
        else:
            self.full_send[step - 2, side, o] = (
                self.own(at, o, pl.ds(0, self.inner))[...] + self.full_recv[step - 3, side, o].astype(F32)
            ).astype(BF16)

    def step(self, step, o):
        for side, (_, sign) in enumerate(self.sides):
            if step > 1:
                self.copy(step - 1, side, o).wait_recv()
            self.fill(step, side, o, lax.rem(self.me + self.n + sign * (self.steps - step + 1), self.n))
            self.copy(step, side, o).start()

    def final(self, o):
        for side in range(2):
            self.copy(self.steps, side, o).wait_recv()
        ref = self.own(self.me, o, pl.ds(0, self.inner))
        last = self.steps - 2
        ref[...] = ref[...] + self.full_recv[last, 0, o].astype(F32) + self.full_recv[last, 1, o].astype(F32)

    def sent(self, o):
        for step in range(1, self.steps + 1):
            for side in range(2):
                self.copy(step, side, o).wait_send()


class Exchange:
    def __init__(self, sems, n, me, to, own, outer, bufs):
        self.sems, self.n, self.me, self.to, self.own = sems, n, me, to, own
        self.send, self.recv = bufs
        self.base = sems.take(n * outer)

    def copy(self, o, k, sent):
        at = lax.rem(self.me + (k if sent else self.n - k), self.n)
        target = self.me if sent else at
        return self.sems.copy(self.send.at[o, at], self.recv.at[o, target], self.base + o * self.n + k, self.to(k))

    def start(self, o):
        self.send[o] = self.own(o, pl.ds(0, self.n))[...].astype(BF16)
        repeat(self.n - 1, lambda k: self.copy(o, k + 1, True).start())

    def final(self, o):
        total = self.own(o, self.me)[...]
        for k in range(1, self.n):
            self.copy(o, k, False).wait_recv()
        for k in range(1, self.n):
            total = total + self.recv[o, lax.rem(self.me + self.n - k, self.n)].astype(F32)
        self.own(o, self.me)[...] = total

    def sent(self, o):
        repeat(self.n - 1, lambda k: self.copy(o, k + 1, True).wait_send())


def kernel(
    dims, cot, dec, enc, pre, ids, counts, fg_out, ig_out, g0, g1, raw, dv, ev, pv, fg, hit, acc, part, xr, bufs, send, recv, local
):
    nx, ny, nz, rcut, ycut, width = dims
    hx = nx // 2
    windows, feats = nx * ny, dv.shape[2]
    layer = lax.axis_index("layer")
    z = lax.axis_index("feat")
    c = lax.rem(layer, 2)
    y = lax.rem(layer // 2, ny)
    x = layer // (2 * ny)
    is_first = x < hx

    def device(x, y, z, c):
        return ((x * ny + y) * 2 + c, z)

    def shifted(at, n, by):
        return lax.rem(at + by, n)

    def first_only(act):
        pl.when(is_first)(lambda: act())

    sibling = device(x, y, z, 1 - c)
    x_peers = [device(shifted(x, nx, k), y, z, c) for k in range(1, nx)]
    y_peers = [device(x, shifted(y, ny, k), z, c) for k in range(1, ny)]
    z_peers = [device(x, y, shifted(z, nz, k), c) for k in range(1, nz)]
    x_sides, y_sides, z_sides = [(to[0], to[-1]) for to in (x_peers, y_peers, z_peers)]
    peers = [sibling] + x_peers + y_peers + z_peers

    own_copies = [
        pltpu.make_async_copy(cot.at[0], g0.at[x, y, z], local.at[0]),
        pltpu.make_async_copy(cot.at[1], g1.at[x, y, z], local.at[1]),
    ]
    for copy in own_copies:
        copy.start()
    barrier = pltpu.get_barrier_semaphore()
    for peer in peers:
        pl.semaphore_signal(barrier, inc=1, device_id=peer, device_id_type=MESH)
    dec_local = pltpu.make_async_copy(dec, raw, local.at[2])
    enc_local = pltpu.make_async_copy(enc, ev.at[c], local.at[3])
    pre_local = pltpu.make_async_copy(pre.at[:, c], pv.at[c], local.at[4])
    for copy in own_copies:
        copy.wait()
    pl.semaphore_wait(barrier, len(peers))

    sems = Semaphores(send, recv)
    rlo, rhi = pl.ds(0, rcut), pl.ds(rcut, width - rcut)
    ylo, zhi = pl.ds(0, ycut), pl.ds(ycut, width - ycut)

    dec1 = sems.copy(dv.at[1, c], dv.at[1, c], sems.take(), sibling)
    dec0 = sems.copy(dv.at[0, c], dv.at[0, c], sems.take(), sibling)
    enc1 = sems.copy(enc, ev.at[c], sems.take(), sibling)
    pre1 = sems.copy(pre.at[:, 1 - c], pv.at[c], sems.take(), sibling)

    def sort_targets(quarter):
        def one(j):
            at = pl.multiple_of((quarter * (feats // 64) + j) * 16, 16)
            dv[1, c, pl.ds(at, 16), :] = raw[pl.ds(at, 16)][:, 1, :]

            @pl.when(is_first)
            def _():
                dv[0, c, pl.ds(at, 16), :] = raw[pl.ds(at, 16)][:, 0, :]

        repeat(feats // 64, one)

    def each_part(step, act):
        if step == 0:
            act(0, z)
        elif step == nz // 2:
            act(nz - 1, shifted(z, nz, nz // 2))
        else:
            repeat(2, lambda j: act(2 * step - 1 + j, lax.rem(z + nz + (2 * j - 1) * step, nz)))

    def all_parts(act):
        for step in range(nz // 2 + 1):
            each_part(step, act)

    def find_blocks():
        ids_here = ids[layer // windows]
        counts_here = jnp.where(is_first, counts[0:1, :], counts[1:2, :]).astype(F32)
        square = (windows, windows)
        diagonal = lax.broadcasted_iota(jnp.int32, square, 0) == lax.broadcasted_iota(jnp.int32, square, 1)
        column = jnp.sum(jnp.where(diagonal, jnp.broadcast_to(counts_here, square), 0.0), axis=1, keepdims=True)
        live_slots = lax.broadcasted_iota(jnp.int32, ids_here.shape, 1).astype(F32) < column
        for side in range(2):
            slot = (lax.rem(layer - c, windows) + side) * nz + z
            for k in range(feats // BLOCK):
                same = (ids_here == slot * (feats // BLOCK) + k) & live_slots
                found = jnp.max(jnp.where(same, 1.0, 0.0), axis=1, keepdims=True)
                hit[side * (feats // BLOCK) + k] = jnp.broadcast_to(found, (windows, BLOCK))

    class Wave:
        def __init__(self, wave):
            rows = pl.ds(wave * STRIP, STRIP)
            self.wave, self.rows = wave, rows
            self.ya = Direct(sems, ny, y, y_peers, lambda i: g1.at[x, i, z, rows, :])
            self.xt = Direct(sems, nx, x, x_peers, lambda i: g0.at[i, y, z, rows, :], lambda to: to < hx)
            self.yc = Direct(sems, ny, y, y_peers, lambda i: g0.at[:, i, z, rows, rhi])
            self.za = Ring(sems, nz, z, *z_sides, lambda i, p, h: g1.at[x, h, i, rows, :], 1)
            self.zd = Ring(sems, nz, z, *z_sides, lambda i, p, h: g0.at[h, y, i, rows, rlo], 1)
            self.zc = Ring(sems, nz, z, *z_sides, lambda i, p, h: g0.at[p, h, i, rows, rhi], nx)
            self.xa = Ring(sems, nx, x, *x_sides, lambda i, p, h: g1.at[i, h, p, rows, :], nz)
            self.yd = Ring(sems, ny, y, *y_sides, lambda i, p, h: g0.at[h, i, p, rows, rlo], nz)
            own = bufs[wave]
            self.y1 = Scatter(
                sems, ny, y, *y_sides, lambda i, o, js: part.at[o, i, js, rows, ylo], nx, nz, own[0:4]
            )
            self.z1 = Scatter(
                sems, nz, z, *z_sides, lambda i, o, js: part.at[o, js, i, rows, zhi], nx, ny, own[4:8]
            )
            self.z2 = Exchange(
                sems, nz, z, lambda k: (layer, shifted(z, nz, k)), lambda o, i: part.at[o, y, i, rows, ylo], nx, own[8:10]
            )
            self.y2 = Exchange(
                sems, ny, y, lambda k: device(x, shifted(y, ny, k), z, c),
                lambda o, i: part.at[o, i, z, rows, zhi], nx, own[10:12],
            )
            self.end_base = sems.take(nx)
            self.fg_base = sems.take()

        def begin(self):
            self.ya.start()
            self.xt.start()

        def gather(self, step):
            if step == 0:
                self.ya.arrived()
            self.za.step(step + 1)
            each_part(step, lambda n, p: self.xa.step(1, n, p))

            def first():
                if step == 0:
                    self.xt.arrived()
                self.zd.step(step + 1)
                each_part(step, lambda n, p: self.yd.step(1, n, p))
                if step == 0:
                    self.yc.start()
                elif step == 1:
                    self.yc.arrived()
                if step > 0:
                    repeat(nx, lambda s: self.zc.step(step, s, s))

            first_only(first)
            if step > 0:
                each_part(step - 1, lambda n, p: self.xa.step(2, n, p))
                first_only(lambda: each_part(step - 1, lambda n, p: self.yd.step(2, n, p)))

        def gather_last(self):
            each_part(nz // 2, lambda n, p: self.xa.step(2, n, p))

            def first():
                each_part(nz // 2, lambda n, p: self.yd.step(2, n, p))
                repeat(nx, lambda s: self.zc.step(nz // 2 + 1, s, s))

            first_only(first)

        def gathered(self):
            all_parts(lambda n, p: self.xa.step(3, n, p))
            first_only(lambda: all_parts(lambda n, p: self.yd.step(3, n, p)))

        def act(self):
            tokens = windows * STRIP

            def one(zz):
                columns = pl.ds(pl.multiple_of(zz * width, 128), width)
                rows1 = g1[:, :, zz, self.rows, :].reshape(tokens, width)
                for side in range(2):
                    term = lax.dot_general(rows1, dv[1, side, :, columns], CONTRACT, preferred_element_type=F32)
                    acc[side] += term

                @pl.when(is_first)
                def _():
                    rows0 = g0[:, :, zz, self.rows, :].reshape(tokens, width)
                    for side in range(2):
                        term = lax.dot_general(rows0, dv[0, side, :, columns], CONTRACT, preferred_element_type=F32)
                        acc[side] += term

            acc[...] = jnp.zeros_like(acc)
            repeat(nz, one)

        def mask(self):
            def one(w):
                at = pl.ds(pl.multiple_of(w * STRIP, STRIP), STRIP)
                for side in range(2):
                    for k in range(feats // BLOCK):
                        lanes = pl.ds(k * BLOCK, BLOCK)
                        found = hit[side * (feats // BLOCK) + k, pl.ds(w, 1), :] > 0.0
                        live = (pv[side, w, self.rows, lanes].astype(F32) > 0.0) & found
                        fg[side, w, self.rows, lanes] = jnp.where(live, acc[side, at, lanes], 0.0).astype(BF16)

            repeat(windows, one)
            self.fg_copy("local").start()
            self.fg_copy("sent").start()

        def fg_copy(self, which):
            rows = self.rows
            if which == "local":
                return pltpu.make_async_copy(fg.at[c, :, rows], fg_out.at[:, c, rows], local.at[5 + self.wave])
            to = c if which == "sent" else 1 - c
            return sems.copy(fg.at[1 - c, :, rows], fg_out.at[:, to, rows], self.fg_base, sibling)

        def partial(self):
            def one(zz):
                at = pl.ds(pl.multiple_of(zz * width, 128), width)
                total = None
                for side in range(2):
                    grads = fg[side, :, self.rows, :].reshape(windows * STRIP, feats)
                    term = lax.dot_general(grads, ev[side, at, :], CONTRACT, preferred_element_type=F32)
                    total = term if total is None else total + term
                part[:, :, zz, self.rows, :] = total.reshape(nx, ny, STRIP, width)

            repeat(nz, one)

        def reduce(self, stage):
            if stage <= nz // 2:
                repeat(nx, lambda o: self.z1.step(stage, o))
                if stage <= ny // 2:
                    repeat(nx, lambda o: self.y1.step(stage, o))
            elif stage == 5:
                def one(o):
                    self.y1.final(o)
                    self.z2.start(o)

                repeat(nx, one)
            elif stage == 6:
                def one(o):
                    self.z1.final(o)
                    self.y2.start(o)

                repeat(nx, one)
            else:
                def one(o):
                    self.z2.final(o)
                    self.y2.final(o)
                    pl.when(o != x)(lambda: self.end_copy(o, True).start())

                repeat(nx, one)
                xr[x, self.rows] = part[x, y, z, self.rows, :]

        def end_copy(self, at, sent):
            index = self.end_base + lax.rem(at + nx - x, nx) if sent else self.end_base + lax.rem(x + nx - at, nx)
            target = xr.at[x if sent else at, self.rows]
            return sems.copy(part.at[at, y, z, self.rows], target, index, device(at, y, z, c))

        def finish(self):
            for k in range(1, nx):
                self.end_copy(shifted(x, nx, k), False).wait_recv()
            for source in range(2):
                total = xr[source * hx, self.rows]
                for k in range(1, hx):
                    total = total + xr[source * hx + k, self.rows]
                ig_out[source, self.rows] = total.astype(BF16)

        def drain(self):
            self.ya.sent()
            self.xt.sent()
            self.za.sent()
            all_parts(self.xa.sent)

            def first():
                self.yc.sent()
                self.zd.sent()
                repeat(nx, lambda s: self.zc.sent(s, s))
                all_parts(self.yd.sent)

            first_only(first)

            def one(o):
                self.y1.sent(o)
                self.z1.sent(o)
                self.z2.sent(o)
                self.y2.sent(o)

            repeat(nx, one)
            for k in range(1, nx):
                self.end_copy(shifted(x, nx, k), True).wait_send()
            self.fg_copy("local").wait()
            self.fg_copy("sent").wait_send()
            self.fg_copy("arrived").wait_recv()

    one, two = Wave(0), Wave(1)
    one.begin()
    for copy in (dec_local, enc_local, pre_local, enc1, pre1):
        copy.start()
    find_blocks()
    one.gather(0)
    dec_local.wait()
    sort_targets(0)
    one.gather(1)
    sort_targets(1)
    one.gather(2)
    two.begin()
    sort_targets(2)
    one.gather(3)
    two.gather(0)
    sort_targets(3)
    dec1.start()
    first_only(dec0.start)
    one.gather(4)
    two.gather(1)
    one.gather_last()
    two.gather(2)
    dec1.wait_recv()
    first_only(dec0.wait_recv)
    pre_local.wait()
    pre1.wait_recv()
    enc_local.wait()
    enc1.wait_recv()
    one.gathered()
    two.gather(3)
    one.act()
    two.gather(4)
    one.mask()
    one.partial()
    one.reduce(1)
    two.gather_last()
    one.reduce(2)
    one.reduce(3)
    two.gathered()
    one.reduce(4)
    two.act()
    two.mask()
    two.partial()
    two.reduce(1)
    one.reduce(5)
    one.reduce(6)
    two.reduce(2)
    one.reduce(7)
    two.reduce(3)
    two.reduce(4)
    one.finish()
    two.reduce(5)
    two.reduce(6)
    two.reduce(7)
    two.finish()
    one.drain()
    two.drain()
    for copy in (dec1, enc1, pre1):
        copy.wait_send()
    first_only(dec0.wait_send)


def scatter_buffers(n, outer, inner, columns):
    few = (2, outer, inner // 2, STRIP, columns)
    full = (n // 2 - 1, 2, outer, inner, STRIP, columns)
    return [pltpu.VMEM(few, BF16)] * 2 + [pltpu.VMEM(full, BF16)] * 2


def body(cotangent, decoder, encoder, preact, block_ids, block_counts):
    nx = ny = SIDE
    nz = lax.axis_size("feat")
    num_layers = decoder.shape[1]
    feats, width = decoder.shape[0], cotangent.shape[2]
    windows = preact.shape[0] // WIN
    rcut, ycut = width - 128, width - 256
    any_ref = pl.BlockSpec(memory_space=pl.ANY)
    vmem_ref = pl.BlockSpec(memory_space=pltpu.VMEM)
    pieces = (nx, ny, nz, ROWS, width)
    bufs = [
        scatter_buffers(ny, nx, nz, ycut)
        + scatter_buffers(nz, nx, ny, width - ycut)
        + [pltpu.VMEM((nx, nz, STRIP, ycut), BF16)] * 2
        + [pltpu.VMEM((nx, ny, STRIP, width - ycut), BF16)] * 2
    ] * WAVES
    fg, ig = pl.pallas_call(
        functools.partial(kernel, (nx, ny, nz, rcut, ycut, width)),
        out_shape=(
            jax.ShapeDtypeStruct((windows, 2, ROWS, feats), BF16),
            jax.ShapeDtypeStruct((num_layers, ROWS, width), BF16),
        ),
        in_specs=[any_ref] * 4 + [vmem_ref] * 2,
        out_specs=(any_ref, vmem_ref),
        scratch_shapes=[
            pltpu.VMEM(pieces, BF16),
            pltpu.VMEM(pieces, BF16),
            pltpu.VMEM((feats, num_layers, nz * width), BF16),
            pltpu.VMEM((num_layers, 2, feats, nz * width), BF16),
            pltpu.VMEM((2, nz * width, feats), BF16),
            pltpu.VMEM((2, windows, ROWS, feats), BF16),
            pltpu.VMEM((2, windows, ROWS, feats), BF16),
            pltpu.VMEM((2 * feats // BLOCK, windows, BLOCK), F32),
            pltpu.VMEM((2, windows * STRIP, feats), F32),
            pltpu.VMEM(pieces, F32),
            pltpu.VMEM((nx, ROWS, width), F32),
            bufs,
            pltpu.SemaphoreType.DMA((512,)),
            pltpu.SemaphoreType.DMA((512,)),
            pltpu.SemaphoreType.DMA((5 + WAVES,)),
        ],
        compiler_params=pltpu.CompilerParams(
            collective_id=0, has_side_effects=True, vmem_limit_bytes=60 * 1024 * 1024
        ),
    )(cotangent, decoder, encoder, preact.reshape(windows, 2, ROWS, feats), block_ids, block_counts)
    return fg.reshape(windows * WIN, feats), ig


def solution(mesh):
    return jax.shard_map(
        body,
        mesh=mesh,
        in_specs=(
            P(None, "layer", "feat"),
            P(("layer", "feat"), None, None),
            P(None, ("layer", "feat")),
            P(None, ("layer", "feat")),
            P(),
            P(),
        ),
        out_specs=(P(None, ("layer", "feat")), P(None, "layer", "feat")),
        check_vma=False,
    )
```

```python
import functools

import jax
import jax.numpy as jnp
from jax import lax
from jax.experimental import pallas as pl
from jax.experimental.pallas import tpu as pltpu
from jax.sharding import PartitionSpec as P

MESH = pl.DeviceIdType.MESH
WIN = 64
ROWS = WIN // 2
WAVES = 2
STRIP = ROWS // WAVES
BLOCK = 128
SIDE = 4
F32 = jnp.float32
BF16 = jnp.bfloat16
WHOLE = pl.ds(0, SIDE)
CONTRACT = (((1,), (1,)), ((), ()))


def half(side):
    return pl.ds(side * (SIDE // 2), SIDE // 2)


def repeat(count, fn):
    if count == 1:
        fn(0)
        return

    def loop(i, carry):
        fn(i)
        return carry

    lax.fori_loop(0, count, loop, 0)


class Semaphores:
    def __init__(self, send, recv):
        self.send, self.recv, self.used = send, recv, 0

    def take(self, count=1):
        first = self.used
        self.used += count
        return first

    def copy(self, source, target, index, device):
        return pltpu.make_async_remote_copy(
            src_ref=source,
            dst_ref=target,
            send_sem=self.send.at[index],
            recv_sem=self.recv.at[index],
            device_id=device,
            device_id_type=MESH,
        )


class Direct:
    def __init__(self, sems, n, me, to, chunk, wanted=None):
        self.sems, self.n, self.me, self.to, self.chunk, self.wanted = sems, n, me, to, chunk, wanted
        self.base = sems.take(n - 1)

    def copy(self, k, sent):
        ref = self.chunk(self.me if sent else lax.rem(self.me + self.n - k, self.n))
        return self.sems.copy(ref, ref, self.base + k - 1, self.to[k - 1])

    def each(self, act):
        for k in range(1, self.n):
            if self.wanted is None:
                act(k)
            else:
                pl.when(self.wanted(lax.rem(self.me + k, self.n)))(lambda k=k: act(k))

    def start(self):
        self.each(lambda k: self.copy(k, True).start())

    def arrived(self):
        for k in range(1, self.n):
            self.copy(k, False).wait_recv()

    def sent(self):
        self.each(lambda k: self.copy(k, True).wait_send())


class Ring:
    def __init__(self, sems, n, me, right, left, chunk, parts):
        self.sems, self.n, self.me, self.sides = sems, n, me, ((right, -1), (left, 1))
        self.chunk, self.parts, self.steps = chunk, parts, n // 2
        self.base = sems.take(2 * self.steps * parts)

    def copies(self, step, number, part, sent):
        found = []
        for side, (device, sign) in enumerate(self.sides):
            at = lax.rem(self.me + self.n + sign * (step - (1 if sent else 0)), self.n)
            ref = self.chunk(at, part, half(side) if step == self.steps else WHOLE)
            index = self.base + (2 * (step - 1) + side) * self.parts + number
            found.append(self.sems.copy(ref, ref, index, device))
        return found

    def step(self, step, number=0, part=0):
        if step > 1:
            for copy in self.copies(step - 1, number, part, False):
                copy.wait_recv()
        if step <= self.steps:
            for copy in self.copies(step, number, part, True):
                copy.start()

    def sent(self, number=0, part=0):
        for step in range(1, self.steps + 1):
            for copy in self.copies(step, number, part, True):
                copy.wait_send()


class Scatter:
    def __init__(self, sems, n, me, right, left, own, outer, inner, bufs):
        self.half_send, self.half_recv, self.full_send, self.full_recv = bufs
        self.sems, self.n, self.me, self.own, self.outer, self.inner = sems, n, me, own, outer, inner
        self.steps = n // 2
        self.sides = ((right, 1), (left, -1))
        self.base = sems.take(2 * self.steps * outer)

    def copy(self, step, side, o):
        index = self.base + ((step - 1) * 2 + side) * self.outer + o
        device = self.sides[side][0]
        if step == 1:
            return self.sems.copy(self.half_send.at[side, o], self.half_recv.at[side, o], index, device)
        return self.sems.copy(self.full_send.at[step - 2, side, o], self.full_recv.at[step - 2, side, o], index, device)

    def fill(self, step, side, o, at):
        count = self.inner // 2
        mine, others = pl.ds(side * count, count), pl.ds((1 - side) * count, count)
        if step == 1:
            self.half_send[side, o] = self.own(at, o, mine)[...].astype(BF16)
        elif step == 2:
            self.full_send[0, side, o, mine] = (
                self.own(at, o, mine)[...] + self.half_recv[side, o].astype(F32)
            ).astype(BF16)
            self.full_send[0, side, o, others] = self.own(at, o, others)[...].astype(BF16)
        else:
            self.full_send[step - 2, side, o] = (
                self.own(at, o, pl.ds(0, self.inner))[...] + self.full_recv[step - 3, side, o].astype(F32)
            ).astype(BF16)

    def step(self, step, o):
        for side, (_, sign) in enumerate(self.sides):
            if step > 1:
                self.copy(step - 1, side, o).wait_recv()
            self.fill(step, side, o, lax.rem(self.me + self.n + sign * (self.steps - step + 1), self.n))
            self.copy(step, side, o).start()

    def final(self, o):
        for side in range(2):
            self.copy(self.steps, side, o).wait_recv()
        ref = self.own(self.me, o, pl.ds(0, self.inner))
        last = self.steps - 2
        ref[...] = ref[...] + self.full_recv[last, 0, o].astype(F32) + self.full_recv[last, 1, o].astype(F32)

    def sent(self, o):
        for step in range(1, self.steps + 1):
            for side in range(2):
                self.copy(step, side, o).wait_send()


class Exchange:
    def __init__(self, sems, n, me, to, own, outer, bufs):
        self.sems, self.n, self.me, self.to, self.own = sems, n, me, to, own
        self.send, self.recv = bufs
        self.base = sems.take(n * outer)

    def copy(self, o, k, sent):
        at = lax.rem(self.me + (k if sent else self.n - k), self.n)
        target = self.me if sent else at
        return self.sems.copy(self.send.at[o, at], self.recv.at[o, target], self.base + o * self.n + k, self.to(k))

    def start(self, o):
        self.send[o] = self.own(o, pl.ds(0, self.n))[...].astype(BF16)
        repeat(self.n - 1, lambda k: self.copy(o, k + 1, True).start())

    def final(self, o):
        total = self.own(o, self.me)[...]
        for k in range(1, self.n):
            self.copy(o, k, False).wait_recv()
        for k in range(1, self.n):
            total = total + self.recv[o, lax.rem(self.me + self.n - k, self.n)].astype(F32)
        self.own(o, self.me)[...] = total

    def sent(self, o):
        repeat(self.n - 1, lambda k: self.copy(o, k + 1, True).wait_send())


def kernel(
    dims, cot, dec, enc, pre, ids, counts, fg_out, ig_out, g0, g1, raw, dv, ev, pv, fg, hit, acc, part, xr, bufs, send, recv, local
):
    nx, ny, nz, rcut, ycut, width = dims
    hx = nx // 2
    windows, feats = nx * ny, dv.shape[2]
    layer = lax.axis_index("layer")
    z = lax.axis_index("feat")
    c = lax.rem(layer, 2)
    y = lax.rem(layer // 2, ny)
    x = layer // (2 * ny)
    is_first = x < hx

    def device(x, y, z, c):
        return ((x * ny + y) * 2 + c, z)

    def shifted(at, n, by):
        return lax.rem(at + by, n)

    def first_only(act):
        pl.when(is_first)(lambda: act())

    sibling = device(x, y, z, 1 - c)
    x_peers = [device(shifted(x, nx, k), y, z, c) for k in range(1, nx)]
    y_peers = [device(x, shifted(y, ny, k), z, c) for k in range(1, ny)]
    z_peers = [device(x, y, shifted(z, nz, k), c) for k in range(1, nz)]
    x_sides, y_sides, z_sides = [(to[0], to[-1]) for to in (x_peers, y_peers, z_peers)]
    peers = [sibling] + x_peers + y_peers + z_peers

    own_copies = [
        pltpu.make_async_copy(cot.at[0], g0.at[x, y, z], local.at[0]),
        pltpu.make_async_copy(cot.at[1], g1.at[x, y, z], local.at[1]),
    ]
    for copy in own_copies:
        copy.start()
    barrier = pltpu.get_barrier_semaphore()
    for peer in peers:
        pl.semaphore_signal(barrier, inc=1, device_id=peer, device_id_type=MESH)
    dec_local = pltpu.make_async_copy(dec, raw, local.at[2])
    enc_local = pltpu.make_async_copy(enc, ev.at[c], local.at[3])
    pre_local = pltpu.make_async_copy(pre.at[:, c], pv.at[c], local.at[4])
    for copy in own_copies:
        copy.wait()
    pl.semaphore_wait(barrier, len(peers))

    sems = Semaphores(send, recv)
    rlo, rhi = pl.ds(0, rcut), pl.ds(rcut, width - rcut)
    ylo, zhi = pl.ds(0, ycut), pl.ds(ycut, width - ycut)

    dec1 = sems.copy(dv.at[1, c], dv.at[1, c], sems.take(), sibling)
    dec0 = sems.copy(dv.at[0, c], dv.at[0, c], sems.take(), sibling)
    enc1 = sems.copy(enc, ev.at[c], sems.take(), sibling)
    pre1 = sems.copy(pre.at[:, 1 - c], pv.at[c], sems.take(), sibling)

    def sort_targets(quarter):
        def one(j):
            at = pl.multiple_of((quarter * (feats // 64) + j) * 16, 16)
            dv[1, c, pl.ds(at, 16), :] = raw[pl.ds(at, 16)][:, 1, :]

            @pl.when(is_first)
            def _():
                dv[0, c, pl.ds(at, 16), :] = raw[pl.ds(at, 16)][:, 0, :]

        repeat(feats // 64, one)

    def each_part(step, act):
        if step == 0:
            act(0, z)
        elif step == nz // 2:
            act(nz - 1, shifted(z, nz, nz // 2))
        else:
            repeat(2, lambda j: act(2 * step - 1 + j, lax.rem(z + nz + (2 * j - 1) * step, nz)))

    def all_parts(act):
        for step in range(nz // 2 + 1):
            each_part(step, act)

    def find_blocks():
        ids_here = ids[layer // windows]
        counts_here = jnp.where(is_first, counts[0:1, :], counts[1:2, :]).astype(F32)
        square = (windows, windows)
        diagonal = lax.broadcasted_iota(jnp.int32, square, 0) == lax.broadcasted_iota(jnp.int32, square, 1)
        column = jnp.sum(jnp.where(diagonal, jnp.broadcast_to(counts_here, square), 0.0), axis=1, keepdims=True)
        live_slots = lax.broadcasted_iota(jnp.int32, ids_here.shape, 1).astype(F32) < column
        for side in range(2):
            slot = (lax.rem(layer - c, windows) + side) * nz + z
            for k in range(feats // BLOCK):
                same = (ids_here == slot * (feats // BLOCK) + k) & live_slots
                found = jnp.max(jnp.where(same, 1.0, 0.0), axis=1, keepdims=True)
                hit[side * (feats // BLOCK) + k] = jnp.broadcast_to(found, (windows, BLOCK))

    class Wave:
        def __init__(self, wave):
            rows = pl.ds(wave * STRIP, STRIP)
            self.wave, self.rows = wave, rows
            self.ya = Direct(sems, ny, y, y_peers, lambda i: g1.at[x, i, z, rows, :])
            self.xt = Direct(sems, nx, x, x_peers, lambda i: g0.at[i, y, z, rows, :], lambda to: to < hx)
            self.yc = Direct(sems, ny, y, y_peers, lambda i: g0.at[:, i, z, rows, rhi])
            self.za = Ring(sems, nz, z, *z_sides, lambda i, p, h: g1.at[x, h, i, rows, :], 1)
            self.zd = Ring(sems, nz, z, *z_sides, lambda i, p, h: g0.at[h, y, i, rows, rlo], 1)
            self.zc = Ring(sems, nz, z, *z_sides, lambda i, p, h: g0.at[p, h, i, rows, rhi], nx)
            self.xa = Ring(sems, nx, x, *x_sides, lambda i, p, h: g1.at[i, h, p, rows, :], nz)
            self.yd = Ring(sems, ny, y, *y_sides, lambda i, p, h: g0.at[h, i, p, rows, rlo], nz)
            own = bufs[wave]
            self.y1 = Scatter(
                sems, ny, y, *y_sides, lambda i, o, js: part.at[o, i, js, rows, ylo], nx, nz, own[0:4]
            )
            self.z1 = Scatter(
                sems, nz, z, *z_sides, lambda i, o, js: part.at[o, js, i, rows, zhi], nx, ny, own[4:8]
            )
            if wave == 0:
                self.z2 = Scatter(
                    sems, nz, z, *z_sides, lambda i, o, js: part.at[js, y, i, rows, ylo], 1, nx, own[8:12]
                )
            else:
                self.z2 = Exchange(
                    sems, nz, z, lambda k: (layer, shifted(z, nz, k)), lambda o, i: part.at[o, y, i, rows, ylo], nx,
                    own[8:10],
                )
            self.y2 = Exchange(
                sems, ny, y, lambda k: device(x, shifted(y, ny, k), z, c),
                lambda o, i: part.at[o, i, z, rows, zhi], nx, own[-2:],
            )
            self.end_base = sems.take(nx)
            self.fg_base = sems.take()

        def begin(self):
            self.ya.start()
            self.xt.start()

        def gather(self, step):
            if step == 0:
                self.ya.arrived()
            self.za.step(step + 1)
            each_part(step, lambda n, p: self.xa.step(1, n, p))

            def first():
                if step == 0:
                    self.xt.arrived()
                self.zd.step(step + 1)
                each_part(step, lambda n, p: self.yd.step(1, n, p))
                if step == 0:
                    self.yc.start()
                elif step == 1:
                    self.yc.arrived()
                if step > 0:
                    repeat(nx, lambda s: self.zc.step(step, s, s))

            first_only(first)
            if step > 0:
                each_part(step - 1, lambda n, p: self.xa.step(2, n, p))
                first_only(lambda: each_part(step - 1, lambda n, p: self.yd.step(2, n, p)))

        def gather_last(self):
            each_part(nz // 2, lambda n, p: self.xa.step(2, n, p))

            def first():
                each_part(nz // 2, lambda n, p: self.yd.step(2, n, p))
                repeat(nx, lambda s: self.zc.step(nz // 2 + 1, s, s))

            first_only(first)

        def act(self, *steps):
            tokens = windows * STRIP

            def term(target, side, at):
                ref = g1 if target else g0
                rows = ref[:, :, at, self.rows, :].reshape(tokens, width)
                columns = pl.ds(pl.multiple_of(at * width, 128), width)
                return lax.dot_general(rows, dv[target, side, :, columns], CONTRACT, preferred_element_type=F32)

            def one(number, at):
                self.xa.step(3, number, at)

                @pl.when(is_first)
                def _():
                    self.yd.step(3, number, at)
                    for side in range(2):
                        acc[side] += term(1, side, at) + term(0, side, at)

                @pl.when(jnp.logical_not(is_first))
                def _():
                    for side in range(2):
                        acc[side] += term(1, side, at)

            for step in steps:
                if step == 0:
                    acc[...] = jnp.zeros_like(acc)
                each_part(step, one)

        def mask(self):
            def one(w):
                at = pl.ds(pl.multiple_of(w * STRIP, STRIP), STRIP)
                for side in range(2):
                    for k in range(feats // BLOCK):
                        lanes = pl.ds(k * BLOCK, BLOCK)
                        found = hit[side * (feats // BLOCK) + k, pl.ds(w, 1), :] > 0.0
                        live = (pv[side, w, self.rows, lanes].astype(F32) > 0.0) & found
                        fg[side, w, self.rows, lanes] = jnp.where(live, acc[side, at, lanes], 0.0).astype(BF16)

            repeat(windows, one)
            self.fg_copy("local").start()
            self.fg_copy("sent").start()

        def fg_copy(self, which):
            rows = self.rows
            if which == "local":
                return pltpu.make_async_copy(fg.at[c, :, rows], fg_out.at[:, c, rows], local.at[5 + self.wave])
            to = c if which == "sent" else 1 - c
            return sems.copy(fg.at[1 - c, :, rows], fg_out.at[:, to, rows], self.fg_base, sibling)

        def partial(self):
            def one(zz):
                at = pl.ds(pl.multiple_of(zz * width, 128), width)
                total = None
                for side in range(2):
                    grads = fg[side, :, self.rows, :].reshape(windows * STRIP, feats)
                    term = lax.dot_general(grads, ev[side, at, :], CONTRACT, preferred_element_type=F32)
                    total = term if total is None else total + term
                part[:, :, zz, self.rows, :] = total.reshape(nx, ny, STRIP, width)

            repeat(nz, one)

        def reduce(self, stage):
            if stage <= nz // 2:
                repeat(nx, lambda o: self.z1.step(stage, o))
                if stage <= ny // 2:
                    repeat(nx, lambda o: self.y1.step(stage, o))
            elif stage == 5:
                def one(o):
                    self.y1.final(o)
                    if self.wave == 1:
                        self.z2.start(o)

                repeat(nx, one)
                if self.wave == 0:
                    self.z2.step(1, 0)
            elif stage == 6:
                def one(o):
                    self.z1.final(o)
                    self.y2.start(o)

                repeat(nx, one)
            else:
                if self.wave == 0:
                    self.z2.final(0)

                def one(o):
                    if self.wave == 1:
                        self.z2.final(o)
                    self.y2.final(o)
                    pl.when(o != x)(lambda: self.end_copy(o, True).start())

                repeat(nx, one)
                xr[x, self.rows] = part[x, y, z, self.rows, :]

        def end_copy(self, at, sent):
            index = self.end_base + lax.rem(at + nx - x, nx) if sent else self.end_base + lax.rem(x + nx - at, nx)
            target = xr.at[x if sent else at, self.rows]
            return sems.copy(part.at[at, y, z, self.rows], target, index, device(at, y, z, c))

        def finish(self):
            for k in range(1, nx):
                self.end_copy(shifted(x, nx, k), False).wait_recv()
            for source in range(2):
                total = xr[source * hx, self.rows]
                for k in range(1, hx):
                    total = total + xr[source * hx + k, self.rows]
                ig_out[source, self.rows] = total.astype(BF16)

        def drain(self):
            self.ya.sent()
            self.xt.sent()
            self.za.sent()
            all_parts(self.xa.sent)

            def first():
                self.yc.sent()
                self.zd.sent()
                repeat(nx, lambda s: self.zc.sent(s, s))
                all_parts(self.yd.sent)

            first_only(first)

            def one(o):
                self.y1.sent(o)
                self.z1.sent(o)
                self.y2.sent(o)
                if self.wave == 1:
                    self.z2.sent(o)

            repeat(nx, one)
            if self.wave == 0:
                self.z2.sent(0)
            for k in range(1, nx):
                self.end_copy(shifted(x, nx, k), True).wait_send()
            self.fg_copy("local").wait()
            self.fg_copy("sent").wait_send()
            self.fg_copy("arrived").wait_recv()

    one, two = Wave(0), Wave(1)
    one.begin()
    for copy in (dec_local, enc_local, pre_local, enc1, pre1):
        copy.start()
    find_blocks()
    one.gather(0)
    dec_local.wait()
    sort_targets(0)
    one.gather(1)
    sort_targets(1)
    one.gather(2)
    two.begin()
    sort_targets(2)
    one.gather(3)
    two.gather(0)
    sort_targets(3)
    dec1.start()
    first_only(dec0.start)
    one.gather(4)
    two.gather(1)
    one.gather_last()
    two.gather(2)
    dec1.wait_recv()
    first_only(dec0.wait_recv)
    pre_local.wait()
    pre1.wait_recv()
    enc_local.wait()
    enc1.wait_recv()
    one.act(0, 1, 2)
    two.gather(3)
    one.act(3, 4)
    two.gather(4)
    one.mask()
    one.partial()
    one.reduce(1)
    two.gather_last()
    two.act(0, 1)
    one.reduce(2)
    two.act(2, 3)
    one.reduce(3)
    two.act(4)
    two.mask()
    one.reduce(4)
    two.partial()
    two.reduce(1)
    one.reduce(5)
    two.reduce(2)
    one.reduce(6)
    one.z2.step(2, 0)
    two.reduce(3)
    one.z2.step(3, 0)
    two.reduce(4)
    one.z2.step(4, 0)
    two.reduce(5)
    one.reduce(7)
    two.reduce(6)
    one.finish()
    two.reduce(7)
    two.finish()
    one.drain()
    two.drain()
    for copy in (dec1, enc1, pre1):
        copy.wait_send()
    first_only(dec0.wait_send)


def scatter_buffers(n, outer, inner, columns):
    few = (2, outer, inner // 2, STRIP, columns)
    full = (n // 2 - 1, 2, outer, inner, STRIP, columns)
    return [pltpu.VMEM(few, BF16)] * 2 + [pltpu.VMEM(full, BF16)] * 2


def body(cotangent, decoder, encoder, preact, block_ids, block_counts):
    nx = ny = SIDE
    nz = lax.axis_size("feat")
    num_layers = decoder.shape[1]
    feats, width = decoder.shape[0], cotangent.shape[2]
    windows = preact.shape[0] // WIN
    rcut, ycut = width - 128, width - 256
    any_ref = pl.BlockSpec(memory_space=pl.ANY)
    vmem_ref = pl.BlockSpec(memory_space=pltpu.VMEM)
    pieces = (nx, ny, nz, ROWS, width)
    common = scatter_buffers(ny, nx, nz, ycut) + scatter_buffers(nz, nx, ny, width - ycut)
    last = [pltpu.VMEM((nx, ny, STRIP, width - ycut), BF16)] * 2
    bufs = [
        common + scatter_buffers(nz, 1, nx, ycut) + last,
        common + [pltpu.VMEM((nx, nz, STRIP, ycut), BF16)] * 2 + last,
    ]
    fg, ig = pl.pallas_call(
        functools.partial(kernel, (nx, ny, nz, rcut, ycut, width)),
        out_shape=(
            jax.ShapeDtypeStruct((windows, 2, ROWS, feats), BF16),
            jax.ShapeDtypeStruct((num_layers, ROWS, width), BF16),
        ),
        in_specs=[any_ref] * 4 + [vmem_ref] * 2,
        out_specs=(any_ref, vmem_ref),
        scratch_shapes=[
            pltpu.VMEM(pieces, BF16),
            pltpu.VMEM(pieces, BF16),
            pltpu.VMEM((feats, num_layers, nz * width), BF16),
            pltpu.VMEM((num_layers, 2, feats, nz * width), BF16),
            pltpu.VMEM((2, nz * width, feats), BF16),
            pltpu.VMEM((2, windows, ROWS, feats), BF16),
            pltpu.VMEM((2, windows, ROWS, feats), BF16),
            pltpu.VMEM((2 * feats // BLOCK, windows, BLOCK), F32),
            pltpu.VMEM((2, windows * STRIP, feats), F32),
            pltpu.VMEM(pieces, F32),
            pltpu.VMEM((nx, ROWS, width), F32),
            bufs,
            pltpu.SemaphoreType.DMA((512,)),
            pltpu.SemaphoreType.DMA((512,)),
            pltpu.SemaphoreType.DMA((5 + WAVES,)),
        ],
        compiler_params=pltpu.CompilerParams(
            collective_id=0, has_side_effects=True, vmem_limit_bytes=60 * 1024 * 1024
        ),
    )(cotangent, decoder, encoder, preact.reshape(windows, 2, ROWS, feats), block_ids, block_counts)
    return fg.reshape(windows * WIN, feats), ig


def solution(mesh):
    return jax.shard_map(
        body,
        mesh=mesh,
        in_specs=(
            P(None, "layer", "feat"),
            P(("layer", "feat"), None, None),
            P(None, ("layer", "feat")),
            P(None, ("layer", "feat")),
            P(),
            P(),
        ),
        out_specs=(P(None, ("layer", "feat")), P(None, "layer", "feat")),
        check_vma=False,
    )
```

```python
import functools

import jax
import jax.numpy as jnp
from jax import lax
from jax.experimental import pallas as pl
from jax.experimental.pallas import tpu as pltpu
from jax.sharding import PartitionSpec as P

MESH = pl.DeviceIdType.MESH
WIN = 64
ROWS = WIN // 2
WAVES = 2
STRIP = ROWS // WAVES
BLOCK = 128
SIDE = 4
F32 = jnp.float32
BF16 = jnp.bfloat16
WHOLE = pl.ds(0, SIDE)
CONTRACT = (((1,), (1,)), ((), ()))


def half(side):
    return pl.ds(side * (SIDE // 2), SIDE // 2)


def repeat(count, fn):
    if count == 1:
        fn(0)
        return

    def loop(i, carry):
        fn(i)
        return carry

    lax.fori_loop(0, count, loop, 0)


class Semaphores:
    def __init__(self, send, recv):
        self.send, self.recv, self.used = send, recv, 0

    def take(self, count=1):
        first = self.used
        self.used += count
        return first

    def copy(self, source, target, index, device):
        return pltpu.make_async_remote_copy(
            src_ref=source,
            dst_ref=target,
            send_sem=self.send.at[index],
            recv_sem=self.recv.at[index],
            device_id=device,
            device_id_type=MESH,
        )


class Direct:
    def __init__(self, sems, n, me, to, chunk, wanted=None):
        self.sems, self.n, self.me, self.to, self.chunk, self.wanted = sems, n, me, to, chunk, wanted
        self.base = sems.take(n - 1)

    def copy(self, k, sent):
        ref = self.chunk(self.me if sent else lax.rem(self.me + self.n - k, self.n))
        return self.sems.copy(ref, ref, self.base + k - 1, self.to[k - 1])

    def each(self, act):
        for k in range(1, self.n):
            if self.wanted is None:
                act(k)
            else:
                pl.when(self.wanted(lax.rem(self.me + k, self.n)))(lambda k=k: act(k))

    def start(self):
        self.each(lambda k: self.copy(k, True).start())

    def arrived(self):
        for k in range(1, self.n):
            self.copy(k, False).wait_recv()

    def sent(self):
        self.each(lambda k: self.copy(k, True).wait_send())


class Ring:
    def __init__(self, sems, n, me, right, left, chunk, parts):
        self.sems, self.n, self.me, self.sides = sems, n, me, ((right, -1), (left, 1))
        self.chunk, self.parts, self.steps = chunk, parts, n // 2
        self.base = sems.take(2 * self.steps * parts)

    def copies(self, step, number, part, sent):
        found = []
        for side, (device, sign) in enumerate(self.sides):
            at = lax.rem(self.me + self.n + sign * (step - (1 if sent else 0)), self.n)
            ref = self.chunk(at, part, half(side) if step == self.steps else WHOLE)
            index = self.base + (2 * (step - 1) + side) * self.parts + number
            found.append(self.sems.copy(ref, ref, index, device))
        return found

    def step(self, step, number=0, part=0):
        if step > 1:
            for copy in self.copies(step - 1, number, part, False):
                copy.wait_recv()
        if step <= self.steps:
            for copy in self.copies(step, number, part, True):
                copy.start()

    def sent(self, number=0, part=0):
        for step in range(1, self.steps + 1):
            for copy in self.copies(step, number, part, True):
                copy.wait_send()


class Scatter:
    def __init__(self, sems, n, me, right, left, own, outer, inner, bufs):
        self.half_send, self.half_recv, self.full_send, self.full_recv = bufs
        self.sems, self.n, self.me, self.own, self.outer, self.inner = sems, n, me, own, outer, inner
        self.steps = n // 2
        self.sides = ((right, 1), (left, -1))
        self.base = sems.take(2 * self.steps * outer)

    def copy(self, step, side, o):
        index = self.base + ((step - 1) * 2 + side) * self.outer + o
        device = self.sides[side][0]
        if step == 1:
            return self.sems.copy(self.half_send.at[side, o], self.half_recv.at[side, o], index, device)
        return self.sems.copy(self.full_send.at[step - 2, side, o], self.full_recv.at[step - 2, side, o], index, device)

    def fill(self, step, side, o, at):
        count = self.inner // 2
        mine, others = pl.ds(side * count, count), pl.ds((1 - side) * count, count)
        if step == 1:
            self.half_send[side, o] = self.own(at, o, mine)[...].astype(BF16)
        elif step == 2:
            self.full_send[0, side, o, mine] = (
                self.own(at, o, mine)[...] + self.half_recv[side, o].astype(F32)
            ).astype(BF16)
            self.full_send[0, side, o, others] = self.own(at, o, others)[...].astype(BF16)
        else:
            self.full_send[step - 2, side, o] = (
                self.own(at, o, pl.ds(0, self.inner))[...] + self.full_recv[step - 3, side, o].astype(F32)
            ).astype(BF16)

    def step(self, step, o):
        for side, (_, sign) in enumerate(self.sides):
            if step > 1:
                self.copy(step - 1, side, o).wait_recv()
            self.fill(step, side, o, lax.rem(self.me + self.n + sign * (self.steps - step + 1), self.n))
            self.copy(step, side, o).start()

    def final(self, o):
        for side in range(2):
            self.copy(self.steps, side, o).wait_recv()
        ref = self.own(self.me, o, pl.ds(0, self.inner))
        last = self.steps - 2
        ref[...] = ref[...] + self.full_recv[last, 0, o].astype(F32) + self.full_recv[last, 1, o].astype(F32)

    def sent(self, o):
        for step in range(1, self.steps + 1):
            for side in range(2):
                self.copy(step, side, o).wait_send()


class Exchange:
    def __init__(self, sems, n, me, to, own, outer, bufs):
        self.sems, self.n, self.me, self.to, self.own = sems, n, me, to, own
        self.send, self.recv = bufs
        self.base = sems.take(n * outer)

    def copy(self, o, k, sent):
        at = lax.rem(self.me + (k if sent else self.n - k), self.n)
        target = self.me if sent else at
        return self.sems.copy(self.send.at[o, at], self.recv.at[o, target], self.base + o * self.n + k, self.to(k))

    def start(self, o):
        self.send[o] = self.own(o, pl.ds(0, self.n))[...].astype(BF16)
        repeat(self.n - 1, lambda k: self.copy(o, k + 1, True).start())

    def final(self, o):
        total = self.own(o, self.me)[...]
        for k in range(1, self.n):
            self.copy(o, k, False).wait_recv()
        for k in range(1, self.n):
            total = total + self.recv[o, lax.rem(self.me + self.n - k, self.n)].astype(F32)
        self.own(o, self.me)[...] = total

    def sent(self, o):
        repeat(self.n - 1, lambda k: self.copy(o, k + 1, True).wait_send())


def kernel(
    dims, cot, dec, enc, pre, ids, counts, fg_out, ig_out, g0, g1, raw, dv, ev, pv, fg, hit, acc, part, xr, bufs, send, recv, local
):
    nx, ny, nz, rcut, ycut, zcut, width = dims
    hx = nx // 2
    windows, feats = nx * ny, dv.shape[2]
    layer = lax.axis_index("layer")
    z = lax.axis_index("feat")
    c = lax.rem(layer, 2)
    y = lax.rem(layer // 2, ny)
    x = layer // (2 * ny)
    is_first = x < hx

    def device(x, y, z, c):
        return ((x * ny + y) * 2 + c, z)

    def shifted(at, n, by):
        return lax.rem(at + by, n)

    def first_only(act):
        pl.when(is_first)(lambda: act())

    sibling = device(x, y, z, 1 - c)
    x_peers = [device(shifted(x, nx, k), y, z, c) for k in range(1, nx)]
    y_peers = [device(x, shifted(y, ny, k), z, c) for k in range(1, ny)]
    z_peers = [device(x, y, shifted(z, nz, k), c) for k in range(1, nz)]
    x_sides, y_sides, z_sides = [(to[0], to[-1]) for to in (x_peers, y_peers, z_peers)]
    peers = [sibling] + x_peers + y_peers + z_peers

    own_copies = [
        pltpu.make_async_copy(cot.at[0], g0.at[x, y, z], local.at[0]),
        pltpu.make_async_copy(cot.at[1], g1.at[x, y, z], local.at[1]),
    ]
    for copy in own_copies:
        copy.start()
    barrier = pltpu.get_barrier_semaphore()
    for peer in peers:
        pl.semaphore_signal(barrier, inc=1, device_id=peer, device_id_type=MESH)
    dec_local = pltpu.make_async_copy(dec, raw, local.at[2])
    enc_local = pltpu.make_async_copy(enc, ev.at[c], local.at[3])
    pre_local = pltpu.make_async_copy(pre.at[:, c], pv.at[c], local.at[4])
    for copy in own_copies:
        copy.wait()
    pl.semaphore_wait(barrier, len(peers))

    sems = Semaphores(send, recv)
    rlo, rhi = pl.ds(0, rcut), pl.ds(rcut, width - rcut)
    ylo, xmid, zhi = pl.ds(0, ycut), pl.ds(ycut, zcut - ycut), pl.ds(zcut, width - zcut)
    partner = device(x + 1 - 2 * lax.rem(x, 2), y, z, c)
    mine, others = lax.rem(x, 2) * hx, (1 - lax.rem(x, 2)) * hx

    dec1 = sems.copy(dv.at[1, c], dv.at[1, c], sems.take(), sibling)
    dec0 = sems.copy(dv.at[0, c], dv.at[0, c], sems.take(), sibling)
    enc1 = sems.copy(enc, ev.at[c], sems.take(), sibling)
    pre1 = sems.copy(pre.at[:, 1 - c], pv.at[c], sems.take(), sibling)

    def sort_targets(quarter):
        def one(j):
            at = pl.multiple_of((quarter * (feats // 64) + j) * 16, 16)
            dv[1, c, pl.ds(at, 16), :] = raw[pl.ds(at, 16)][:, 1, :]

            @pl.when(is_first)
            def _():
                dv[0, c, pl.ds(at, 16), :] = raw[pl.ds(at, 16)][:, 0, :]

        repeat(feats // 64, one)

    def each_part(step, act):
        if step == 0:
            act(0, z)
        elif step == nz // 2:
            act(nz - 1, shifted(z, nz, nz // 2))
        else:
            repeat(2, lambda j: act(2 * step - 1 + j, lax.rem(z + nz + (2 * j - 1) * step, nz)))

    def all_parts(act):
        for step in range(nz // 2 + 1):
            each_part(step, act)

    def find_blocks():
        ids_here = ids[layer // windows]
        counts_here = jnp.where(is_first, counts[0:1, :], counts[1:2, :]).astype(F32)
        square = (windows, windows)
        diagonal = lax.broadcasted_iota(jnp.int32, square, 0) == lax.broadcasted_iota(jnp.int32, square, 1)
        column = jnp.sum(jnp.where(diagonal, jnp.broadcast_to(counts_here, square), 0.0), axis=1, keepdims=True)
        live_slots = lax.broadcasted_iota(jnp.int32, ids_here.shape, 1).astype(F32) < column
        for side in range(2):
            slot = (lax.rem(layer - c, windows) + side) * nz + z
            for k in range(feats // BLOCK):
                same = (ids_here == slot * (feats // BLOCK) + k) & live_slots
                found = jnp.max(jnp.where(same, 1.0, 0.0), axis=1, keepdims=True)
                hit[side * (feats // BLOCK) + k] = jnp.broadcast_to(found, (windows, BLOCK))

    class Wave:
        def __init__(self, wave):
            rows = pl.ds(wave * STRIP, STRIP)
            self.wave, self.rows = wave, rows
            self.ya = Direct(sems, ny, y, y_peers, lambda i: g1.at[x, i, z, rows, :])
            self.xt = Direct(sems, nx, x, x_peers, lambda i: g0.at[i, y, z, rows, :], lambda to: to < hx)
            self.yc = Direct(sems, ny, y, y_peers, lambda i: g0.at[:, i, z, rows, rhi])
            self.za = Ring(sems, nz, z, *z_sides, lambda i, p, h: g1.at[x, h, i, rows, :], 1)
            self.zd = Ring(sems, nz, z, *z_sides, lambda i, p, h: g0.at[h, y, i, rows, rlo], 1)
            self.zc = Ring(sems, nz, z, *z_sides, lambda i, p, h: g0.at[p, h, i, rows, rhi], nx)
            self.xa = Ring(sems, nx, x, *x_sides, lambda i, p, h: g1.at[i, h, p, rows, :], nz)
            self.yd = Ring(sems, ny, y, *y_sides, lambda i, p, h: g0.at[h, i, p, rows, rlo], nz)
            own = bufs[wave]
            self.y1 = Scatter(
                sems, ny, y, *y_sides, lambda i, o, js: part.at[o, i, js, rows, ylo], nx, nz, own[0:4]
            )
            self.z1 = Scatter(
                sems, nz, z, *z_sides, lambda i, o, js: part.at[o, js, i, rows, zhi], nx, ny, own[4:8]
            )
            if wave == 0:
                self.z2 = Scatter(
                    sems, nz, z, *z_sides, lambda i, o, js: part.at[js, y, i, rows, ylo], 1, nx, own[8:12]
                )
            else:
                self.z2 = Exchange(
                    sems, nz, z, lambda k: (layer, shifted(z, nz, k)), lambda o, i: part.at[o, y, i, rows, ylo], nx,
                    own[8:10],
                )
            self.y2 = Exchange(
                sems, ny, y, lambda k: device(x, shifted(y, ny, k), z, c),
                lambda o, i: part.at[o, i, z, rows, zhi], nx, own[-2:],
            )
            self.pair_send, self.pair_recv = own[-4:-2]
            self.pair_base = sems.take(hx)
            self.y3 = Scatter(
                sems, ny, y, *y_sides, lambda i, o, js: part.at[mine + o, i, js, rows, xmid], hx, nz, own[-8:-4]
            )
            self.z3 = Exchange(
                sems, nz, z, lambda k: (layer, shifted(z, nz, k)), lambda o, i: part.at[mine + o, y, i, rows, xmid], hx,
                own[-10:-8],
            )
            self.end_base = sems.take(nx)
            self.fg_base = sems.take()

        def begin(self):
            self.ya.start()
            self.xt.start()

        def gather(self, step):
            if step == 0:
                self.ya.arrived()
            self.za.step(step + 1)
            each_part(step, lambda n, p: self.xa.step(1, n, p))

            def first():
                if step == 0:
                    self.xt.arrived()
                self.zd.step(step + 1)
                each_part(step, lambda n, p: self.yd.step(1, n, p))
                if step == 0:
                    self.yc.start()
                elif step == 1:
                    self.yc.arrived()
                if step > 0:
                    repeat(nx, lambda s: self.zc.step(step, s, s))

            first_only(first)
            if step > 0:
                each_part(step - 1, lambda n, p: self.xa.step(2, n, p))
                first_only(lambda: each_part(step - 1, lambda n, p: self.yd.step(2, n, p)))

        def gather_last(self):
            each_part(nz // 2, lambda n, p: self.xa.step(2, n, p))

            def first():
                each_part(nz // 2, lambda n, p: self.yd.step(2, n, p))
                repeat(nx, lambda s: self.zc.step(nz // 2 + 1, s, s))

            first_only(first)

        def act(self, *steps):
            tokens = windows * STRIP

            def term(target, side, at):
                ref = g1 if target else g0
                rows = ref[:, :, at, self.rows, :].reshape(tokens, width)
                columns = pl.ds(pl.multiple_of(at * width, 128), width)
                return lax.dot_general(rows, dv[target, side, :, columns], CONTRACT, preferred_element_type=F32)

            def one(number, at):
                self.xa.step(3, number, at)

                @pl.when(is_first)
                def _():
                    self.yd.step(3, number, at)
                    for side in range(2):
                        acc[side] += term(1, side, at) + term(0, side, at)

                @pl.when(jnp.logical_not(is_first))
                def _():
                    for side in range(2):
                        acc[side] += term(1, side, at)

            for step in steps:
                if step == 0:
                    acc[...] = jnp.zeros_like(acc)
                each_part(step, one)

        def mask(self):
            def one(w):
                at = pl.ds(pl.multiple_of(w * STRIP, STRIP), STRIP)
                for side in range(2):
                    for k in range(feats // BLOCK):
                        lanes = pl.ds(k * BLOCK, BLOCK)
                        found = hit[side * (feats // BLOCK) + k, pl.ds(w, 1), :] > 0.0
                        live = (pv[side, w, self.rows, lanes].astype(F32) > 0.0) & found
                        fg[side, w, self.rows, lanes] = jnp.where(live, acc[side, at, lanes], 0.0).astype(BF16)

            repeat(windows, one)
            self.fg_copy("local").start()
            self.fg_copy("sent").start()

        def fg_copy(self, which):
            rows = self.rows
            if which == "local":
                return pltpu.make_async_copy(fg.at[c, :, rows], fg_out.at[:, c, rows], local.at[5 + self.wave])
            to = c if which == "sent" else 1 - c
            return sems.copy(fg.at[1 - c, :, rows], fg_out.at[:, to, rows], self.fg_base, sibling)

        def partial(self):
            def one(zz):
                at = pl.ds(pl.multiple_of(zz * width, 128), width)
                total = None
                for side in range(2):
                    grads = fg[side, :, self.rows, :].reshape(windows * STRIP, feats)
                    term = lax.dot_general(grads, ev[side, at, :], CONTRACT, preferred_element_type=F32)
                    total = term if total is None else total + term
                part[:, :, zz, self.rows, :] = total.reshape(nx, ny, STRIP, width)

            repeat(nz, one)

        def pair_copy(self, o):
            return sems.copy(self.pair_send.at[o], self.pair_recv.at[o], self.pair_base + o, partner)

        def pair_start(self, o):
            self.pair_send[o] = part[others + o, :, :, self.rows, xmid].astype(BF16)
            self.pair_copy(o).start()

        def pair_final(self, o):
            self.pair_copy(o).wait_recv()
            part[mine + o, :, :, self.rows, xmid] = (
                part[mine + o, :, :, self.rows, xmid] + self.pair_recv[o].astype(F32)
            )
            self.y3.step(1, o)

        def reduce(self, stage):
            if stage == 1:
                repeat(hx, self.pair_start)
            if stage <= nz // 2:
                repeat(nx, lambda o: self.z1.step(stage, o))
                if stage <= ny // 2:
                    repeat(nx, lambda o: self.y1.step(stage, o))
                elif stage == 3:
                    repeat(hx, self.pair_final)
                else:
                    repeat(hx, lambda o: self.y3.step(2, o))
            elif stage == 5:
                def one(o):
                    self.y1.final(o)
                    if self.wave == 1:
                        self.z2.start(o)

                repeat(nx, one)
                if self.wave == 0:
                    self.z2.step(1, 0)
            elif stage == 6:
                def third(o):
                    self.y3.final(o)
                    self.z3.start(o)

                def one(o):
                    self.z1.final(o)
                    self.y2.start(o)

                repeat(hx, third)
                repeat(nx, one)
            else:
                repeat(hx, self.z3.final)
                if self.wave == 0:
                    self.z2.final(0)

                def one(o):
                    if self.wave == 1:
                        self.z2.final(o)
                    self.y2.final(o)
                    pl.when(o != x)(lambda: self.end_copy(o, True).start())

                repeat(nx, one)
                xr[x, self.rows] = part[x, y, z, self.rows, :]

        def end_copy(self, at, sent):
            index = self.end_base + lax.rem(at + nx - x, nx) if sent else self.end_base + lax.rem(x + nx - at, nx)
            target = xr.at[x if sent else at, self.rows]
            return sems.copy(part.at[at, y, z, self.rows], target, index, device(at, y, z, c))

        def finish(self):
            for k in range(1, nx):
                self.end_copy(shifted(x, nx, k), False).wait_recv()
            for source in range(2):
                total = xr[source * hx, self.rows]
                for k in range(1, hx):
                    total = total + xr[source * hx + k, self.rows]
                ig_out[source, self.rows] = total.astype(BF16)
                ig_out[source, self.rows, xmid] = xr[source * hx + x // hx, self.rows, xmid].astype(BF16)

        def drain(self):
            self.ya.sent()
            self.xt.sent()
            self.za.sent()
            all_parts(self.xa.sent)

            def first():
                self.yc.sent()
                self.zd.sent()
                repeat(nx, lambda s: self.zc.sent(s, s))
                all_parts(self.yd.sent)

            first_only(first)

            def one(o):
                self.y1.sent(o)
                self.z1.sent(o)
                self.y2.sent(o)
                if self.wave == 1:
                    self.z2.sent(o)

            def pair(o):
                self.pair_copy(o).wait_send()
                self.y3.sent(o)
                self.z3.sent(o)

            repeat(nx, one)
            repeat(hx, pair)
            if self.wave == 0:
                self.z2.sent(0)
            for k in range(1, nx):
                self.end_copy(shifted(x, nx, k), True).wait_send()
            self.fg_copy("local").wait()
            self.fg_copy("sent").wait_send()
            self.fg_copy("arrived").wait_recv()

    one, two = Wave(0), Wave(1)
    one.begin()
    for copy in (dec_local, enc_local, pre_local, enc1, pre1):
        copy.start()
    find_blocks()
    one.gather(0)
    two.begin()
    dec_local.wait()
    sort_targets(0)
    one.gather(1)
    sort_targets(1)
    one.gather(2)
    two.gather(0)
    sort_targets(2)
    one.gather(3)
    two.gather(1)
    sort_targets(3)
    dec1.start()
    first_only(dec0.start)
    one.gather(4)
    two.gather(2)
    one.gather_last()
    dec1.wait_recv()
    first_only(dec0.wait_recv)
    pre_local.wait()
    pre1.wait_recv()
    enc_local.wait()
    enc1.wait_recv()
    one.act(0, 1, 2)
    two.gather(3)
    one.act(3, 4)
    two.gather(4)
    one.mask()
    one.partial()
    one.reduce(1)
    two.gather_last()
    two.act(0, 1)
    one.reduce(2)
    two.act(2, 3)
    one.reduce(3)
    two.act(4)
    two.mask()
    one.reduce(4)
    two.partial()
    two.reduce(1)
    one.reduce(5)
    two.reduce(2)
    one.reduce(6)
    one.z2.step(2, 0)
    two.reduce(3)
    one.z2.step(3, 0)
    two.reduce(4)
    one.z2.step(4, 0)
    two.reduce(5)
    one.reduce(7)
    two.reduce(6)
    one.finish()
    two.reduce(7)
    two.finish()
    one.drain()
    two.drain()
    for copy in (dec1, enc1, pre1):
        copy.wait_send()
    first_only(dec0.wait_send)


def scatter_buffers(n, outer, inner, columns):
    few = (2, outer, inner // 2, STRIP, columns)
    full = (n // 2 - 1, 2, outer, inner, STRIP, columns)
    return [pltpu.VMEM(few, BF16)] * 2 + [pltpu.VMEM(full, BF16)] * 2


def body(cotangent, decoder, encoder, preact, block_ids, block_counts):
    nx = ny = SIDE
    nz = lax.axis_size("feat")
    num_layers = decoder.shape[1]
    feats, width = decoder.shape[0], cotangent.shape[2]
    windows = preact.shape[0] // WIN
    rcut, ycut, zcut = width - 128, width - 384, width - 256
    any_ref = pl.BlockSpec(memory_space=pl.ANY)
    vmem_ref = pl.BlockSpec(memory_space=pltpu.VMEM)
    pieces = (nx, ny, nz, ROWS, width)
    common = scatter_buffers(ny, nx, nz, ycut) + scatter_buffers(nz, nx, ny, width - zcut)
    hx, middle = nx // 2, zcut - ycut
    last = (
        [pltpu.VMEM((hx, nz, STRIP, middle), BF16)] * 2
        + scatter_buffers(ny, hx, nz, middle)
        + [pltpu.VMEM((hx, ny, nz, STRIP, middle), BF16)] * 2
        + [pltpu.VMEM((nx, ny, STRIP, width - zcut), BF16)] * 2
    )
    bufs = [
        common + scatter_buffers(nz, 1, nx, ycut) + last,
        common + [pltpu.VMEM((nx, nz, STRIP, ycut), BF16)] * 2 + last,
    ]
    fg, ig = pl.pallas_call(
        functools.partial(kernel, (nx, ny, nz, rcut, ycut, zcut, width)),
        out_shape=(
            jax.ShapeDtypeStruct((windows, 2, ROWS, feats), BF16),
            jax.ShapeDtypeStruct((num_layers, ROWS, width), BF16),
        ),
        in_specs=[any_ref] * 4 + [vmem_ref] * 2,
        out_specs=(any_ref, vmem_ref),
        scratch_shapes=[
            pltpu.VMEM(pieces, BF16),
            pltpu.VMEM(pieces, BF16),
            pltpu.VMEM((feats, num_layers, nz * width), BF16),
            pltpu.VMEM((num_layers, 2, feats, nz * width), BF16),
            pltpu.VMEM((2, nz * width, feats), BF16),
            pltpu.VMEM((2, windows, ROWS, feats), BF16),
            pltpu.VMEM((2, windows, ROWS, feats), BF16),
            pltpu.VMEM((2 * feats // BLOCK, windows, BLOCK), F32),
            pltpu.VMEM((2, windows * STRIP, feats), F32),
            pltpu.VMEM(pieces, F32),
            pltpu.VMEM((nx, ROWS, width), F32),
            bufs,
            pltpu.SemaphoreType.DMA((560,)),
            pltpu.SemaphoreType.DMA((560,)),
            pltpu.SemaphoreType.DMA((5 + WAVES,)),
        ],
        compiler_params=pltpu.CompilerParams(
            collective_id=0, has_side_effects=True, vmem_limit_bytes=60 * 1024 * 1024
        ),
    )(cotangent, decoder, encoder, preact.reshape(windows, 2, ROWS, feats), block_ids, block_counts)
    return fg.reshape(windows * WIN, feats), ig


def solution(mesh):
    return jax.shard_map(
        body,
        mesh=mesh,
        in_specs=(
            P(None, "layer", "feat"),
            P(("layer", "feat"), None, None),
            P(None, ("layer", "feat")),
            P(None, ("layer", "feat")),
            P(),
            P(),
        ),
        out_specs=(P(None, ("layer", "feat")), P(None, "layer", "feat")),
        check_vma=False,
    )
```

```python
import functools

import jax
import jax.numpy as jnp
from jax import lax
from jax.experimental import pallas as pl
from jax.experimental.pallas import tpu as pltpu
from jax.sharding import PartitionSpec as P

MESH = pl.DeviceIdType.MESH
WIN = 64
ROWS = WIN // 2
WAVES = 2
STRIP = ROWS // WAVES
BLOCK = 128
SIDE = 4
F32 = jnp.float32
BF16 = jnp.bfloat16
WHOLE = pl.ds(0, SIDE)
CONTRACT = (((1,), (1,)), ((), ()))


def half(side):
    return pl.ds(side * (SIDE // 2), SIDE // 2)


def repeat(count, fn):
    if count == 1:
        fn(0)
        return

    def loop(i, carry):
        fn(i)
        return carry

    lax.fori_loop(0, count, loop, 0)


class Semaphores:
    def __init__(self, send, recv):
        self.send, self.recv, self.used = send, recv, 0

    def take(self, count=1):
        first = self.used
        self.used += count
        return first

    def copy(self, source, target, index, device):
        return pltpu.make_async_remote_copy(
            src_ref=source,
            dst_ref=target,
            send_sem=self.send.at[index],
            recv_sem=self.recv.at[index],
            device_id=device,
            device_id_type=MESH,
        )


class Direct:
    def __init__(self, sems, n, me, to, chunk, wanted=None):
        self.sems, self.n, self.me, self.to, self.chunk, self.wanted = sems, n, me, to, chunk, wanted
        self.base = sems.take(n - 1)

    def copy(self, k, sent):
        ref = self.chunk(self.me if sent else lax.rem(self.me + self.n - k, self.n))
        return self.sems.copy(ref, ref, self.base + k - 1, self.to[k - 1])

    def each(self, act):
        for k in range(1, self.n):
            if self.wanted is None:
                act(k)
            else:
                pl.when(self.wanted(lax.rem(self.me + k, self.n)))(lambda k=k: act(k))

    def start(self):
        self.each(lambda k: self.copy(k, True).start())

    def arrived(self):
        for k in range(1, self.n):
            self.copy(k, False).wait_recv()

    def sent(self):
        self.each(lambda k: self.copy(k, True).wait_send())


class Ring:
    def __init__(self, sems, n, me, right, left, chunk, parts):
        self.sems, self.n, self.me, self.sides = sems, n, me, ((right, -1), (left, 1))
        self.chunk, self.parts, self.steps = chunk, parts, n // 2
        self.base = sems.take(2 * self.steps * parts)

    def copies(self, step, number, part, sent):
        found = []
        for side, (device, sign) in enumerate(self.sides):
            at = lax.rem(self.me + self.n + sign * (step - (1 if sent else 0)), self.n)
            ref = self.chunk(at, part, half(side) if step == self.steps else WHOLE)
            index = self.base + (2 * (step - 1) + side) * self.parts + number
            found.append(self.sems.copy(ref, ref, index, device))
        return found

    def step(self, step, number=0, part=0):
        if step > 1:
            for copy in self.copies(step - 1, number, part, False):
                copy.wait_recv()
        if step <= self.steps:
            for copy in self.copies(step, number, part, True):
                copy.start()

    def sent(self, number=0, part=0):
        for step in range(1, self.steps + 1):
            for copy in self.copies(step, number, part, True):
                copy.wait_send()


class Scatter:
    def __init__(self, sems, n, me, right, left, own, outer, inner, bufs):
        self.half_send, self.half_recv, self.full_send, self.full_recv = bufs
        self.sems, self.n, self.me, self.own, self.outer, self.inner = sems, n, me, own, outer, inner
        self.steps = n // 2
        self.sides = ((right, 1), (left, -1))
        self.base = sems.take(2 * self.steps * outer)

    def copy(self, step, side, o):
        index = self.base + ((step - 1) * 2 + side) * self.outer + o
        device = self.sides[side][0]
        if step == 1:
            return self.sems.copy(self.half_send.at[side, o], self.half_recv.at[side, o], index, device)
        return self.sems.copy(self.full_send.at[step - 2, side, o], self.full_recv.at[step - 2, side, o], index, device)

    def fill(self, step, side, o, at):
        count = self.inner // 2
        mine, others = pl.ds(side * count, count), pl.ds((1 - side) * count, count)
        if step == 1:
            self.half_send[side, o] = self.own(at, o, mine)[...].astype(BF16)
        elif step == 2:
            self.full_send[0, side, o, mine] = (
                self.own(at, o, mine)[...] + self.half_recv[side, o].astype(F32)
            ).astype(BF16)
            self.full_send[0, side, o, others] = self.own(at, o, others)[...].astype(BF16)
        else:
            self.full_send[step - 2, side, o] = (
                self.own(at, o, pl.ds(0, self.inner))[...] + self.full_recv[step - 3, side, o].astype(F32)
            ).astype(BF16)

    def step(self, step, o):
        for side, (_, sign) in enumerate(self.sides):
            if step > 1:
                self.copy(step - 1, side, o).wait_recv()
            self.fill(step, side, o, lax.rem(self.me + self.n + sign * (self.steps - step + 1), self.n))
            self.copy(step, side, o).start()

    def final(self, o):
        for side in range(2):
            self.copy(self.steps, side, o).wait_recv()
        ref = self.own(self.me, o, pl.ds(0, self.inner))
        last = self.steps - 2
        ref[...] = ref[...] + self.full_recv[last, 0, o].astype(F32) + self.full_recv[last, 1, o].astype(F32)

    def sent(self, o):
        for step in range(1, self.steps + 1):
            for side in range(2):
                self.copy(step, side, o).wait_send()


class Exchange:
    def __init__(self, sems, n, me, to, own, outer, bufs):
        self.sems, self.n, self.me, self.to, self.own = sems, n, me, to, own
        self.send, self.recv = bufs
        self.base = sems.take(n * outer)

    def copy(self, o, k, sent):
        at = lax.rem(self.me + (k if sent else self.n - k), self.n)
        target = self.me if sent else at
        return self.sems.copy(self.send.at[o, at], self.recv.at[o, target], self.base + o * self.n + k, self.to(k))

    def start(self, o):
        self.send[o] = self.own(o, pl.ds(0, self.n))[...].astype(BF16)
        repeat(self.n - 1, lambda k: self.copy(o, k + 1, True).start())

    def final(self, o):
        total = self.own(o, self.me)[...]
        for k in range(1, self.n):
            self.copy(o, k, False).wait_recv()
        for k in range(1, self.n):
            total = total + self.recv[o, lax.rem(self.me + self.n - k, self.n)].astype(F32)
        self.own(o, self.me)[...] = total

    def sent(self, o):
        repeat(self.n - 1, lambda k: self.copy(o, k + 1, True).wait_send())


def kernel(
    dims, cot, dec, enc, pre, ids, counts, fg_out, ig_out, g0, g1, raw, dv, ev, pv, fg, hit, acc, part, xr, bufs, send, recv, local
):
    nx, ny, nz, rcut, ycut, width = dims
    hx = nx // 2
    windows, feats = nx * ny, dv.shape[2]
    layer = lax.axis_index("layer")
    z = lax.axis_index("feat")
    c = lax.rem(layer, 2)
    y = lax.rem(layer // 2, ny)
    x = layer // (2 * ny)
    is_first = x < hx

    def device(x, y, z, c):
        return ((x * ny + y) * 2 + c, z)

    def shifted(at, n, by):
        return lax.rem(at + by, n)

    def first_only(act):
        pl.when(is_first)(lambda: act())

    sibling = device(x, y, z, 1 - c)
    x_peers = [device(shifted(x, nx, k), y, z, c) for k in range(1, nx)]
    y_peers = [device(x, shifted(y, ny, k), z, c) for k in range(1, ny)]
    z_peers = [device(x, y, shifted(z, nz, k), c) for k in range(1, nz)]
    x_sides, y_sides, z_sides = [(to[0], to[-1]) for to in (x_peers, y_peers, z_peers)]
    peers = [sibling] + x_peers + y_peers + z_peers

    own_copies = [
        pltpu.make_async_copy(cot.at[0], g0.at[x, y, z], local.at[0]),
        pltpu.make_async_copy(cot.at[1], g1.at[x, y, z], local.at[1]),
    ]
    for copy in own_copies:
        copy.start()
    barrier = pltpu.get_barrier_semaphore()
    for peer in peers:
        pl.semaphore_signal(barrier, inc=1, device_id=peer, device_id_type=MESH)
    dec_local = pltpu.make_async_copy(dec, raw, local.at[2])
    enc_local = pltpu.make_async_copy(enc, ev.at[c], local.at[3])
    pre_local = pltpu.make_async_copy(pre.at[:, c], pv.at[c], local.at[4])
    for copy in own_copies:
        copy.wait()
    pl.semaphore_wait(barrier, len(peers))

    sems = Semaphores(send, recv)
    rlo, rhi = pl.ds(0, rcut), pl.ds(rcut, width - rcut)
    ylo, zhi = pl.ds(0, ycut), pl.ds(ycut, width - ycut)

    dec1 = sems.copy(dv.at[1, c], dv.at[1, c], sems.take(), sibling)
    dec0 = sems.copy(dv.at[0, c], dv.at[0, c], sems.take(), sibling)
    enc1 = sems.copy(enc, ev.at[c], sems.take(), sibling)
    pre1 = sems.copy(pre.at[:, 1 - c], pv.at[c], sems.take(), sibling)

    def sort_targets(quarter):
        def one(j):
            at = pl.multiple_of((quarter * (feats // 64) + j) * 16, 16)
            dv[1, c, pl.ds(at, 16), :] = raw[pl.ds(at, 16)][:, 1, :]

            @pl.when(is_first)
            def _():
                dv[0, c, pl.ds(at, 16), :] = raw[pl.ds(at, 16)][:, 0, :]

        repeat(feats // 64, one)

    def each_part(step, act):
        if step == 0:
            act(0, z)
        elif step == nz // 2:
            act(nz - 1, shifted(z, nz, nz // 2))
        else:
            repeat(2, lambda j: act(2 * step - 1 + j, lax.rem(z + nz + (2 * j - 1) * step, nz)))

    def all_parts(act):
        for step in range(nz // 2 + 1):
            each_part(step, act)

    def find_blocks():
        ids_here = ids[layer // windows]
        counts_here = jnp.where(is_first, counts[0:1, :], counts[1:2, :]).astype(F32)
        square = (windows, windows)
        diagonal = lax.broadcasted_iota(jnp.int32, square, 0) == lax.broadcasted_iota(jnp.int32, square, 1)
        column = jnp.sum(jnp.where(diagonal, jnp.broadcast_to(counts_here, square), 0.0), axis=1, keepdims=True)
        live_slots = lax.broadcasted_iota(jnp.int32, ids_here.shape, 1).astype(F32) < column
        for side in range(2):
            slot = (lax.rem(layer - c, windows) + side) * nz + z
            for k in range(feats // BLOCK):
                same = (ids_here == slot * (feats // BLOCK) + k) & live_slots
                found = jnp.max(jnp.where(same, 1.0, 0.0), axis=1, keepdims=True)
                hit[side * (feats // BLOCK) + k] = jnp.broadcast_to(found, (windows, BLOCK))

    class Wave:
        def __init__(self, wave):
            rows = pl.ds(wave * STRIP, STRIP)
            self.wave, self.rows = wave, rows
            self.ya = Direct(sems, ny, y, y_peers, lambda i: g1.at[x, i, z, rows, :])
            self.xt = Direct(sems, nx, x, x_peers, lambda i: g0.at[i, y, z, rows, :], lambda to: to < hx)
            self.yc = Direct(sems, ny, y, y_peers, lambda i: g0.at[:, i, z, rows, rhi])
            self.za = Ring(sems, nz, z, *z_sides, lambda i, p, h: g1.at[x, h, i, rows, :], 1)
            self.zd = Ring(sems, nz, z, *z_sides, lambda i, p, h: g0.at[h, y, i, rows, rlo], 1)
            self.zc = Ring(sems, nz, z, *z_sides, lambda i, p, h: g0.at[p, h, i, rows, rhi], nx)
            self.xa = Ring(sems, nx, x, *x_sides, lambda i, p, h: g1.at[i, h, p, rows, :], nz)
            self.yd = Ring(sems, ny, y, *y_sides, lambda i, p, h: g0.at[h, i, p, rows, rlo], nz)
            own = bufs[wave]
            self.y1 = Scatter(
                sems, ny, y, *y_sides, lambda i, o, js: part.at[o, i, js, rows, ylo], nx, nz, own[0:4]
            )
            self.z1 = Scatter(
                sems, nz, z, *z_sides, lambda i, o, js: part.at[o, js, i, rows, zhi], nx, ny, own[4:8]
            )
            if wave == 0:
                self.z2 = Scatter(
                    sems, nz, z, *z_sides, lambda i, o, js: part.at[js, y, i, rows, ylo], 1, nx, own[8:12]
                )
            else:
                self.z2 = Exchange(
                    sems, nz, z, lambda k: (layer, shifted(z, nz, k)), lambda o, i: part.at[o, y, i, rows, ylo], nx,
                    own[8:10],
                )
            self.y2 = Exchange(
                sems, ny, y, lambda k: device(x, shifted(y, ny, k), z, c),
                lambda o, i: part.at[o, i, z, rows, zhi], nx, own[-2:],
            )
            self.end_base = sems.take(nx)
            self.fg_base = sems.take()

        def begin(self):
            self.ya.start()
            self.xt.start()

        def gather(self, step):
            if step == 0:
                self.ya.arrived()
            self.za.step(step + 1)
            each_part(step, lambda n, p: self.xa.step(1, n, p))

            def first():
                if step == 0:
                    self.xt.arrived()
                self.zd.step(step + 1)
                each_part(step, lambda n, p: self.yd.step(1, n, p))
                if step == 0:
                    self.yc.start()
                elif step == 1:
                    self.yc.arrived()
                if step > 0:
                    repeat(nx, lambda s: self.zc.step(step, s, s))

            first_only(first)
            if step > 0:
                each_part(step - 1, lambda n, p: self.xa.step(2, n, p))
                first_only(lambda: each_part(step - 1, lambda n, p: self.yd.step(2, n, p)))

        def gather_last(self):
            each_part(nz // 2, lambda n, p: self.xa.step(2, n, p))

            def first():
                each_part(nz // 2, lambda n, p: self.yd.step(2, n, p))
                repeat(nx, lambda s: self.zc.step(nz // 2 + 1, s, s))

            first_only(first)

        def act(self, *steps):
            tokens = windows * STRIP

            def term(target, side, at):
                ref = g1 if target else g0
                rows = ref[:, :, at, self.rows, :].reshape(tokens, width)
                columns = pl.ds(pl.multiple_of(at * width, 128), width)
                return lax.dot_general(rows, dv[target, side, :, columns], CONTRACT, preferred_element_type=F32)

            def one(number, at):
                self.xa.step(3, number, at)

                @pl.when(is_first)
                def _():
                    self.yd.step(3, number, at)
                    for side in range(2):
                        acc[side] += term(1, side, at) + term(0, side, at)

                @pl.when(jnp.logical_not(is_first))
                def _():
                    for side in range(2):
                        acc[side] += term(1, side, at)

            for step in steps:
                if step == 0:
                    acc[...] = jnp.zeros_like(acc)
                each_part(step, one)

        def mask(self):
            def one(w):
                at = pl.ds(pl.multiple_of(w * STRIP, STRIP), STRIP)
                for side in range(2):
                    for k in range(feats // BLOCK):
                        lanes = pl.ds(k * BLOCK, BLOCK)
                        found = hit[side * (feats // BLOCK) + k, pl.ds(w, 1), :] > 0.0
                        live = (pv[side, w, self.rows, lanes].astype(F32) > 0.0) & found
                        fg[side, w, self.rows, lanes] = jnp.where(live, acc[side, at, lanes], 0.0).astype(BF16)

            repeat(windows, one)
            self.fg_copy("local").start()
            self.fg_copy("sent").start()

        def fg_copy(self, which):
            rows = self.rows
            if which == "local":
                return pltpu.make_async_copy(fg.at[c, :, rows], fg_out.at[:, c, rows], local.at[5 + self.wave])
            to = c if which == "sent" else 1 - c
            return sems.copy(fg.at[1 - c, :, rows], fg_out.at[:, to, rows], self.fg_base, sibling)

        def partial(self):
            def one(zz):
                at = pl.ds(pl.multiple_of(zz * width, 128), width)
                total = None
                for side in range(2):
                    grads = fg[side, :, self.rows, :].reshape(windows * STRIP, feats)
                    term = lax.dot_general(grads, ev[side, at, :], CONTRACT, preferred_element_type=F32)
                    total = term if total is None else total + term
                part[:, :, zz, self.rows, :] = total.reshape(nx, ny, STRIP, width)

            repeat(nz, one)

        def reduce(self, stage):
            if stage <= nz // 2:
                repeat(nx, lambda o: self.z1.step(stage, o))
                if stage <= ny // 2:
                    repeat(nx, lambda o: self.y1.step(stage, o))
            elif stage == 5:
                def one(o):
                    self.y1.final(o)
                    if self.wave == 1:
                        self.z2.start(o)

                repeat(nx, one)
                if self.wave == 0:
                    self.z2.step(1, 0)
            elif stage == 6:
                def one(o):
                    self.z1.final(o)
                    self.y2.start(o)

                repeat(nx, one)
            else:
                if self.wave == 0:
                    self.z2.final(0)

                def one(o):
                    if self.wave == 1:
                        self.z2.final(o)
                    self.y2.final(o)
                    pl.when(o != x)(lambda: self.end_copy(o, True).start())

                repeat(nx, one)
                xr[x, self.rows] = part[x, y, z, self.rows, :]

        def end_copy(self, at, sent):
            index = self.end_base + lax.rem(at + nx - x, nx) if sent else self.end_base + lax.rem(x + nx - at, nx)
            target = xr.at[x if sent else at, self.rows]
            return sems.copy(part.at[at, y, z, self.rows], target, index, device(at, y, z, c))

        def finish(self):
            for k in range(1, nx):
                self.end_copy(shifted(x, nx, k), False).wait_recv()
            for source in range(2):
                total = xr[source * hx, self.rows]
                for k in range(1, hx):
                    total = total + xr[source * hx + k, self.rows]
                ig_out[source, self.rows] = total.astype(BF16)

        def gather_sent(self):
            self.ya.sent()
            self.xt.sent()
            self.za.sent()
            all_parts(self.xa.sent)

            def first():
                self.yc.sent()
                self.zd.sent()
                repeat(nx, lambda s: self.zc.sent(s, s))
                all_parts(self.yd.sent)

            first_only(first)
            self.fg_copy("local").wait()
            self.fg_copy("sent").wait_send()
            self.fg_copy("arrived").wait_recv()

        def rings_sent(self):
            def one(o):
                self.y1.sent(o)
                self.z1.sent(o)

            repeat(nx, one)

        def rest_sent(self):
            repeat(nx, self.y2.sent)
            if self.wave == 0:
                self.z2.sent(0)
            else:
                repeat(nx, self.z2.sent)
            for k in range(1, nx):
                self.end_copy(shifted(x, nx, k), True).wait_send()

    one, two = Wave(0), Wave(1)
    one.begin()
    for copy in (dec_local, enc_local, pre_local, enc1, pre1):
        copy.start()
    find_blocks()
    one.gather(0)
    two.begin()
    dec_local.wait()
    sort_targets(0)
    one.gather(1)
    sort_targets(1)
    one.gather(2)
    two.gather(0)
    sort_targets(2)
    one.gather(3)
    two.gather(1)
    sort_targets(3)
    dec1.start()
    first_only(dec0.start)
    one.gather(4)
    two.gather(2)
    one.gather_last()
    dec1.wait_recv()
    first_only(dec0.wait_recv)
    pre_local.wait()
    pre1.wait_recv()
    enc_local.wait()
    enc1.wait_recv()
    one.act(0, 1, 2)
    two.gather(3)
    one.act(3, 4)
    two.gather(4)
    one.mask()
    one.partial()
    one.reduce(1)
    two.gather_last()
    two.act(0, 1)
    one.reduce(2)
    two.act(2, 3)
    one.reduce(3)
    two.act(4)
    two.mask()
    one.reduce(4)
    two.partial()
    two.reduce(1)
    one.gather_sent()
    one.reduce(5)
    two.reduce(2)
    one.reduce(6)
    one.z2.step(2, 0)
    two.reduce(3)
    one.z2.step(3, 0)
    two.reduce(4)
    two.gather_sent()
    one.z2.step(4, 0)
    two.reduce(5)
    one.reduce(7)
    two.reduce(6)
    one.finish()
    one.rings_sent()
    two.rings_sent()
    two.reduce(7)
    two.finish()
    one.rest_sent()
    two.rest_sent()
    for copy in (dec1, enc1, pre1):
        copy.wait_send()
    first_only(dec0.wait_send)


def scatter_buffers(n, outer, inner, columns):
    few = (2, outer, inner // 2, STRIP, columns)
    full = (n // 2 - 1, 2, outer, inner, STRIP, columns)
    return [pltpu.VMEM(few, BF16)] * 2 + [pltpu.VMEM(full, BF16)] * 2


def body(cotangent, decoder, encoder, preact, block_ids, block_counts):
    nx = ny = SIDE
    nz = lax.axis_size("feat")
    num_layers = decoder.shape[1]
    feats, width = decoder.shape[0], cotangent.shape[2]
    windows = preact.shape[0] // WIN
    rcut, ycut = width - 128, width - 256
    any_ref = pl.BlockSpec(memory_space=pl.ANY)
    vmem_ref = pl.BlockSpec(memory_space=pltpu.VMEM)
    pieces = (nx, ny, nz, ROWS, width)
    common = scatter_buffers(ny, nx, nz, ycut) + scatter_buffers(nz, nx, ny, width - ycut)
    last = [pltpu.VMEM((nx, ny, STRIP, width - ycut), BF16)] * 2
    bufs = [
        common + scatter_buffers(nz, 1, nx, ycut) + last,
        common + [pltpu.VMEM((nx, nz, STRIP, ycut), BF16)] * 2 + last,
    ]
    fg, ig = pl.pallas_call(
        functools.partial(kernel, (nx, ny, nz, rcut, ycut, width)),
        out_shape=(
            jax.ShapeDtypeStruct((windows, 2, ROWS, feats), BF16),
            jax.ShapeDtypeStruct((num_layers, ROWS, width), BF16),
        ),
        in_specs=[any_ref] * 4 + [vmem_ref] * 2,
        out_specs=(any_ref, vmem_ref),
        scratch_shapes=[
            pltpu.VMEM(pieces, BF16),
            pltpu.VMEM(pieces, BF16),
            pltpu.VMEM((feats, num_layers, nz * width), BF16),
            pltpu.VMEM((num_layers, 2, feats, nz * width), BF16),
            pltpu.VMEM((2, nz * width, feats), BF16),
            pltpu.VMEM((2, windows, ROWS, feats), BF16),
            pltpu.VMEM((2, windows, ROWS, feats), BF16),
            pltpu.VMEM((2 * feats // BLOCK, windows, BLOCK), F32),
            pltpu.VMEM((2, windows * STRIP, feats), F32),
            pltpu.VMEM(pieces, F32),
            pltpu.VMEM((nx, ROWS, width), F32),
            bufs,
            pltpu.SemaphoreType.DMA((512,)),
            pltpu.SemaphoreType.DMA((512,)),
            pltpu.SemaphoreType.DMA((5 + WAVES,)),
        ],
        compiler_params=pltpu.CompilerParams(
            collective_id=0, has_side_effects=True, vmem_limit_bytes=60 * 1024 * 1024
        ),
    )(cotangent, decoder, encoder, preact.reshape(windows, 2, ROWS, feats), block_ids, block_counts)
    return fg.reshape(windows * WIN, feats), ig


def solution(mesh):
    return jax.shard_map(
        body,
        mesh=mesh,
        in_specs=(
            P(None, "layer", "feat"),
            P(("layer", "feat"), None, None),
            P(None, ("layer", "feat")),
            P(None, ("layer", "feat")),
            P(),
            P(),
        ),
        out_specs=(P(None, ("layer", "feat")), P(None, "layer", "feat")),
        check_vma=False,
    )
```
